32 devices in a mesh: expert: 4 (over y, x), shard: 8 (over z, core).
Axes of the slice: x: 2, y: 2, z: 4, core: 2. Of those that a mesh axis runs over, the one named last changes fastest.
Arguments:
- tokens_in: bfloat16 [32768, 768], P(('expert', 'shard')), may hold values from -6 to 6
- cotangent: bfloat16 [32768, 768], P(('expert', 'shard'))
- routes: int32 [32768, 2], P(('expert', 'shard')), may hold values from 0 to 3, all different within a row
- prefix: int32 [32], P(('expert', 'shard')), may hold values from 102 to 512
- owners: int32 [48], replicated, may hold values from 0 to 3, as said below
- attn_master: float32 [96, 384, 128], P('expert', 'shard')
- attn_first: float32 [96, 384, 128], P('expert', 'shard')
- attn_second: float32 [96, 384, 128], P('expert', 'shard')
- expert_master: float32 [4, 3, 12288, 128], P('expert', None, 'shard')
- expert_first: float32 [4, 3, 12288, 128], P('expert', None, 'shard')
- expert_second: float32 [4, 3, 12288, 128], P('expert', None, 'shard')
- shared_master: float32 [3, 12288, 128], P(None, ('expert', 'shard'))
- shared_first: float32 [3, 12288, 128], P(None, ('expert', 'shard'))
- shared_second: float32 [3, 12288, 128], P(None, ('expert', 'shard'))
- norm_gains: float32 [2, 768], replicated, may hold values from 0.5 to 1.5
- gains_first: float32 [2, 768], replicated
- gains_second: float32 [2, 768], replicated
- router: float32 [768, 4], replicated, may hold values from -0.15625 to 0.15625
- router_first: float32 [768, 4], replicated
- router_second: float32 [768, 4], replicated
Outputs:
- block_out: bfloat16 [32768, 768], P(('expert', 'shard'))
- tokens_grad: float32 [32768, 768], P(('expert', 'shard'))
- attn_new: float32 [96, 384, 128], P('expert', 'shard')
- attn_first_new: float32 [96, 384, 128], P('expert', 'shard')
- attn_second_new: float32 [96, 384, 128], P('expert', 'shard')
- attn_copy: bfloat16 [48, 384, 128], P(None, 'shard')
- expert_new: float32 [4, 3, 12288, 128], P('expert', None, 'shard')
- expert_first_new: float32 [4, 3, 12288, 128], P('expert', None, 'shard')
- expert_second_new: float32 [4, 3, 12288, 128], P('expert', None, 'shard')
- shared_new: float32 [3, 12288, 128], P(None, ('expert', 'shard'))
- shared_first_new: float32 [3, 12288, 128], P(None, ('expert', 'shard'))
- shared_second_new: float32 [3, 12288, 128], P(None, ('expert', 'shard'))
- gains_new: float32 [2, 768], replicated
- gains_first_new: float32 [2, 768], replicated
- gains_second_new: float32 [2, 768], replicated
- router_new: float32 [768, 4], replicated
- router_first_new: float32 [768, 4], replicated
- router_second_new: float32 [768, 4], replicated
The draws below stay inside these ranges and needn't reach their ends.
Inputs may be any that keep to these rules, and one draw needn't show every extreme that they name: `owners`: no owner holds more than 24 attention matrices, and one holds exactly 24. `routes`: the 2 experts of a token differ.
All inputs are finite; a program needn't handle non-finite values.
Results may differ from the reference program's by a relative error of at most 0.018.
Values may be sent and summed in bfloat16 or wider, within the bound.
No kernel may reach another device: no remote copies, remote signals or barrier semaphores. Data moves between devices by JAX's collectives and lax.ppermute only.
A program may use at most 384 MiB of HBM per device.

```python
import math
import jax
import jax.numpy as jnp
from jax import lax

D = 768
HEADS = 12
HEAD_DIM = 64
FF = 2048
FFS = 2048
TOP = 2
SEQ_LEN = 1024
STEP = 5
EXPERTS = 4
TOK_DEV = 1024
TOKENS = 32768
SEQS = 32
CAP = 512
NMAT = 48
OWN_MAX = 24
SLOTS = 96
ROWS_A = 384
ROWS_E = 12288
ROWS_S = 12288
N_EXPERT = 4
N_SHARD = 8
DEVICES = 32


def owner_table(key):
    key = jax.random.fold_in(key, 501)
    busy_key, spread_key, order_key = jax.random.split(key, 3)
    busiest = jax.random.randint(busy_key, (), 0, N_EXPERT)
    others = jax.random.permutation(spread_key, (N_EXPERT - 1) * OWN_MAX)[:NMAT - OWN_MAX]
    spread_owner = (busiest + 1 + others // OWN_MAX) % N_EXPERT
    owner_list = jnp.concatenate([jnp.full((OWN_MAX,), busiest, jnp.int32), spread_owner.astype(jnp.int32)])
    return owner_list[jax.random.permutation(order_key, NMAT)]


def slot_place_drawn(owner_list):
    onehot = (owner_list[:, None] == jnp.arange(N_EXPERT, dtype=jnp.int32)[None, :]).astype(jnp.int32)
    prior_count = jnp.sum((jnp.cumsum(onehot, 0) - onehot) * onehot, 1)
    return owner_list * OWN_MAX + prior_count


def slot_scales(key, lead_scale, out_scale, empty_scale):
    slot_of = slot_place_drawn(owner_table(key))
    kind_of = jnp.arange(NMAT) // HEADS
    per_matrix = jnp.where(kind_of == 3, out_scale, lead_scale).astype(jnp.float32)
    return jnp.full((SLOTS,), empty_scale, jnp.float32).at[slot_of].set(per_matrix)


def first_moment(key, shape, size):
    return size * jax.random.normal(key, shape, jnp.float32)


def second_moment(key, shape, size):
    return size * size * jnp.exp(jax.random.uniform(key, shape, jnp.float32, 0.0, math.log(4.0)))


def draw_owners(key, part):
    return owner_table(key)


def draw_cotangent(key, part):
    key = jax.random.fold_in(key, 23)
    device_of = jnp.arange(TOKENS) // TOK_DEV
    expert_pos = (device_of // N_SHARD).astype(jnp.float32) / max(N_EXPERT - 1, 1)
    shard_pos = (device_of % N_SHARD).astype(jnp.float32) / max(N_SHARD - 1, 1)
    values = jax.random.truncated_normal(key, -4.0, 4.0, (TOKENS, D), jnp.float32)
    row_scale = jnp.power(3.0, expert_pos + shard_pos) / 3.0
    return (values * row_scale[:, None]).astype(jnp.bfloat16)


def draw_attn_master(key, part):
    per_slot = slot_scales(key, D ** (-0.5), (64.0 / D) ** 0.5, D ** (-0.5))
    key = jax.random.fold_in(key, 11)
    return jax.random.truncated_normal(key, -4.0, 4.0, (SLOTS, ROWS_A, 128), jnp.float32) * per_slot[:, None, None]


def draw_attn_first(key, part):
    root = TOKENS ** 0.5
    per_slot = slot_scales(key, 0.7 * root, 0.1 * root, 0.7 * root)
    key = jax.random.fold_in(key, 12)
    return first_moment(key, (SLOTS, ROWS_A, 128), per_slot[:, None, None])


def draw_attn_second(key, part):
    root = TOKENS ** 0.5
    per_slot = slot_scales(key, 0.7 * root, 0.1 * root, 0.7 * root)
    key = jax.random.fold_in(key, 13)
    return second_moment(key, (SLOTS, ROWS_A, 128), per_slot[:, None, None])


def draw_expert_master(key, part):
    key = jax.random.fold_in(key, 31)
    kind_scale = jnp.array([D ** (-0.5), D ** (-0.5), (3.0 / FF) ** 0.5], jnp.float32)
    return jax.random.truncated_normal(key, -4.0, 4.0, (EXPERTS, 3, ROWS_E, 128), jnp.float32) * kind_scale[None, :, None, None]


def draw_expert_first(key, part):
    key = jax.random.fold_in(key, 32)
    root = (TOKENS * TOP / EXPERTS) ** 0.5
    kind_scale = jnp.array([0.5 * root, 0.5 * root, 0.3 * root], jnp.float32)
    return first_moment(key, (EXPERTS, 3, ROWS_E, 128), kind_scale[None, :, None, None])


def draw_expert_second(key, part):
    key = jax.random.fold_in(key, 33)
    root = (TOKENS * TOP / EXPERTS) ** 0.5
    kind_scale = jnp.array([0.5 * root, 0.5 * root, 0.3 * root], jnp.float32)
    return second_moment(key, (EXPERTS, 3, ROWS_E, 128), kind_scale[None, :, None, None])


def draw_shared_master(key, part):
    key = jax.random.fold_in(key, 41)
    kind_scale = jnp.array([D ** (-0.5), D ** (-0.5), (3.0 / FFS) ** 0.5], jnp.float32)
    return jax.random.truncated_normal(key, -4.0, 4.0, (3, ROWS_S, 128), jnp.float32) * kind_scale[:, None, None]


def draw_shared_first(key, part):
    key = jax.random.fold_in(key, 42)
    root = TOKENS ** 0.5
    kind_scale = jnp.array([root, root, 0.6 * root], jnp.float32)
    return first_moment(key, (3, ROWS_S, 128), kind_scale[:, None, None])


def draw_shared_second(key, part):
    key = jax.random.fold_in(key, 43)
    root = TOKENS ** 0.5
    kind_scale = jnp.array([root, root, 0.6 * root], jnp.float32)
    return second_moment(key, (3, ROWS_S, 128), kind_scale[:, None, None])


def draw_gains_first(key, part):
    key = jax.random.fold_in(key, 51)
    root = TOKENS ** 0.5
    row_size = jnp.array([root, 3.0 * root], jnp.float32)
    return first_moment(key, (2, D), row_size[:, None])


def draw_gains_second(key, part):
    key = jax.random.fold_in(key, 52)
    root = TOKENS ** 0.5
    row_size = jnp.array([root, 3.0 * root], jnp.float32)
    return second_moment(key, (2, D), row_size[:, None])


def draw_router_first(key, part):
    key = jax.random.fold_in(key, 61)
    return first_moment(key, (D, EXPERTS), 9.0 * (TOKENS * TOP / EXPERTS) ** 0.5)


def draw_router_second(key, part):
    key = jax.random.fold_in(key, 62)
    return second_moment(key, (D, EXPERTS), 9.0 * (TOKENS * TOP / EXPERTS) ** 0.5)


def touch_ends(drawn, rng, smallest, high):
    longest = drawn.shape.index(max(drawn.shape))
    spots = []
    for shift in (0, 1):
        where = [jax.random.randint(jax.random.fold_in(rng, axis), (), 0, length) for axis, length in enumerate(drawn.shape)]
        where[longest] = (where[longest] + shift) % drawn.shape[longest]
        spots.append(tuple(where))
    return drawn.at[spots[0]].set(smallest).at[spots[1]].set(high)


def block_scale(rng, dims, shards, smallest, high):
    def one(position, shards_of):
        steps = jax.random.uniform(jax.random.fold_in(jax.random.fold_in(rng, 6), position), (shards_of,), jnp.float32, smallest / len(shards), high / len(shards))
        return jnp.repeat(jnp.exp(steps), dims[position] // shards_of).reshape((-1,) + (1,) * (len(dims) - position - 1))

    gain = one(*shards[0])
    for cut in shards[1:]:
        gain = gain * one(*cut)
    return gain


def choose_distinct(stream_key, rows, count, top, lift):
    order = jax.random.permutation(jax.random.fold_in(stream_key, 1), count)
    pull = order
    for power in range(3):
        pull = pull * pull // count
    pull = pull * lift // count
    tickets = jax.random.randint(jax.random.fold_in(stream_key, 2), (rows, count), 0, 4096) + pull
    sure = jax.random.permutation(jax.random.fold_in(stream_key, 3), rows)[jnp.arange(count) % rows]
    tickets = jnp.where(jnp.arange(rows)[:, None] == sure[None, :], 1 << 14, tickets)
    merit = tickets * count + jnp.arange(count)
    return lax.top_k(merit.astype(jnp.int32), top)[1].astype(jnp.int32)


def gaussian(stream_key, shape, spread, bound, cuts=(), kind=jnp.bfloat16):
    gain = block_scale(stream_key, shape, cuts, -0.22, 0.18) if cuts else 1.0
    values = jax.random.normal(stream_key, shape, jnp.float32) * spread * gain
    return jnp.minimum(jnp.maximum(values, -bound), bound).astype(kind)


def setup_inputs(seed: int = 0) -> dict:
    keys = jax.random.split(jax.random.key(seed), 21)
    tokens_in = gaussian(keys[0], (TOKENS, D), 1.0, 6.0, ((0, 32),))
    cotangent = draw_cotangent(jax.random.fold_in(keys[20], 71), 0)
    routes = choose_distinct(keys[2], TOKENS, EXPERTS, TOP, 4096)
    prefix = touch_ends(jax.random.randint(keys[3], (SEQS,), SEQ_LEN // 10, SEQ_LEN // 2 + 1), jax.random.fold_in(keys[3], 1), SEQ_LEN // 10, (SEQ_LEN // 2 + 1) - 1).astype(jnp.int32)
    owners = draw_owners(jax.random.fold_in(keys[20], 71), 0)
    attn_master = draw_attn_master(jax.random.fold_in(keys[20], 71), 0)
    attn_first = draw_attn_first(jax.random.fold_in(keys[20], 71), 0)
    attn_second = draw_attn_second(jax.random.fold_in(keys[20], 71), 0)
    expert_master = draw_expert_master(jax.random.fold_in(keys[20], 71), 0)
    expert_first = draw_expert_first(jax.random.fold_in(keys[20], 71), 0)
    expert_second = draw_expert_second(jax.random.fold_in(keys[20], 71), 0)
    shared_master = draw_shared_master(jax.random.fold_in(keys[20], 71), 0)
    shared_first = draw_shared_first(jax.random.fold_in(keys[20], 71), 0)
    shared_second = draw_shared_second(jax.random.fold_in(keys[20], 71), 0)
    norm_gains = jnp.clip(1.0 + 0.1 * jax.random.normal(keys[14], (2, D), jnp.float32), 0.5, 1.5)
    gains_first = draw_gains_first(jax.random.fold_in(keys[20], 71), 0)
    gains_second = draw_gains_second(jax.random.fold_in(keys[20], 71), 0)
    router = gaussian(keys[17], (D, EXPERTS), (2 * D) ** -0.5, 0.15625, (), jnp.float32)
    router_first = draw_router_first(jax.random.fold_in(keys[20], 71), 0)
    router_second = draw_router_second(jax.random.fold_in(keys[20], 71), 0)
    return {"tokens_in": tokens_in, "cotangent": cotangent, "routes": routes, "prefix": prefix, "owners": owners, "attn_master": attn_master, "attn_first": attn_first, "attn_second": attn_second, "expert_master": expert_master, "expert_first": expert_first, "expert_second": expert_second, "shared_master": shared_master, "shared_first": shared_first, "shared_second": shared_second, "norm_gains": norm_gains, "gains_first": gains_first, "gains_second": gains_second, "router": router, "router_first": router_first, "router_second": router_second}


NORM_EPSILON = 1e-06
ADAM_EPSILON = 1e-08
FIRST_BETA = 0.5
SECOND_BETA = 0.5
WEIGHT_DECAY = 0.1
RATE_ATTENTION = 0.06
RATE_MATRIX = 0.03
RATE_ROUTER = 0.02
RATE_GAIN = 0.3
ROPE_BASE = 10000.0
HIGHEST = lax.Precision.HIGHEST

@jax.custom_vjp
def low(v):
    return lax.optimization_barrier(v.astype(jnp.bfloat16)).astype(jnp.float32)

@jax.custom_vjp
def low_back(v):
    return v

def low_keep(v):
    return (low(v), None)

def low_pass(kept, grad):
    return (grad,)

def back_keep(v):
    return (v, None)

def back_low(kept, grad):
    return (low(grad),)
low.defvjp(low_keep, low_pass)
low_back.defvjp(back_keep, back_low)

def slot_place(owners):
    onehot = (owners[:, None] == jnp.arange(N_EXPERT, dtype=jnp.int32)[None, :]).astype(jnp.int32)
    prior_count = lax.optimization_barrier(jnp.sum((jnp.cumsum(onehot, 0) - onehot) * onehot, 1))
    return (owners * OWN_MAX + prior_count).astype(jnp.int32)

def rope_tables():
    half_dim = HEAD_DIM // 2
    inv_freq = ROPE_BASE ** (-(jnp.arange(half_dim, dtype=jnp.float32) * 2.0 / HEAD_DIM))
    phase_angle = jnp.arange(SEQ_LEN, dtype=jnp.float32)[:, None] * inv_freq[None, :]
    return (jnp.cos(phase_angle), jnp.sin(phase_angle))

def rotate(values, cos_part, sin_part):
    half_dim = values.shape[-1] // 2
    lead_half = values[..., :half_dim]
    tail_half = values[..., half_dim:]
    cos_wide = cos_part[:, None, :]
    sin_wide = sin_part[:, None, :]
    return jnp.concatenate([lead_half * cos_wide - tail_half * sin_wide, tail_half * cos_wide + lead_half * sin_wide], -1)

def mix_sequence(w_qkv, w_out, w_sgu, w_sd, gains_all, cos_table, sin_table, hidden_seq, prefix_len):
    normed = low(hidden_seq * lax.rsqrt(lax.optimization_barrier(jnp.mean(hidden_seq * hidden_seq, -1, keepdims=True)) + NORM_EPSILON) * gains_all[0])
    qkv = jnp.dot(normed, w_qkv, precision=HIGHEST)
    query_pre = low_back(qkv[:, :D]).reshape(SEQ_LEN, HEADS, HEAD_DIM)
    key_pre = low_back(qkv[:, D:2 * D]).reshape(SEQ_LEN, HEADS, HEAD_DIM)
    value_rows = low(low_back(qkv[:, 2 * D:])).reshape(SEQ_LEN, HEADS, HEAD_DIM)
    query_rot = low(rotate(query_pre, cos_table, sin_table))
    key_rot = low(rotate(key_pre, cos_table, sin_table))
    scores = low_back(jnp.einsum('qhd,khd->hqk', query_rot, key_rot, precision=HIGHEST) * HEAD_DIM ** (-0.5))
    positions = jnp.arange(SEQ_LEN, dtype=jnp.int32)
    allowed = (positions[None, :] <= positions[:, None]) | (positions[None, :] < prefix_len)
    masked = jnp.where(allowed[None], scores, -1e+30)
    exp_scores = jnp.exp(masked - lax.optimization_barrier(jnp.max(masked, -1, keepdims=True)))
    probs = exp_scores / lax.optimization_barrier(jnp.sum(exp_scores, -1, keepdims=True))
    heads_out = low(low_back(jnp.einsum('hqk,khd->qhd', low(probs), value_rows, precision=HIGHEST)))
    attn_out = low_back(jnp.dot(heads_out.reshape(SEQ_LEN, D), w_out, precision=HIGHEST))
    middle = hidden_seq + attn_out
    branch_in = low(middle * lax.rsqrt(lax.optimization_barrier(jnp.mean(middle * middle, -1, keepdims=True)) + NORM_EPSILON) * gains_all[1])
    gate_up = low_back(jnp.dot(branch_in, w_sgu, precision=HIGHEST))
    gate_part = gate_up[:, :FFS]
    shared_hidden = low(gate_part * jax.nn.sigmoid(gate_part) * gate_up[:, FFS:])
    shared_out = low_back(jnp.dot(shared_hidden, w_sd, precision=HIGHEST))
    return (middle, branch_in, shared_out)

def expert_block(expert_args):
    rows, w_gate, w_up, w_down = expert_args
    gate_part = low_back(jnp.dot(rows, w_gate, precision=HIGHEST))
    up_part = low_back(jnp.dot(rows, w_up, precision=HIGHEST))
    expert_hidden = low(gate_part * jax.nn.sigmoid(gate_part) * up_part)
    return low(low_back(jnp.dot(expert_hidden, w_down, precision=HIGHEST)))

def adam_update(weight, first_state, second_state, gradient, step_rate, decay_rate):
    first_new = FIRST_BETA * first_state + (1.0 - FIRST_BETA) * gradient
    second_new = SECOND_BETA * second_state + (1.0 - SECOND_BETA) * gradient * gradient
    first_hat = first_new / (1.0 - FIRST_BETA ** STEP)
    second_hat = second_new / (1.0 - SECOND_BETA ** STEP)
    weight_new = weight - step_rate * (first_hat / (jnp.sqrt(second_hat) + ADAM_EPSILON) + decay_rate * weight)
    return (weight_new, first_new, second_new)

def reference(tokens_in, cotangent, routes, prefix, owners, attn_master, attn_first, attn_second, expert_master, expert_first, expert_second, shared_master, shared_first, shared_second, norm_gains, gains_first, gains_second, router, router_first, router_second):
    slot_of = slot_place(owners)
    ids_dev = routes.reshape(DEVICES, TOK_DEV * TOP)
    onehot = (ids_dev[:, :, None] == jnp.arange(EXPERTS, dtype=jnp.int32)[None, None, :]).astype(jnp.int32)
    slot_rank = lax.optimization_barrier(jnp.sum((jnp.cumsum(onehot, 1) - onehot) * onehot, 2))
    device_of = jnp.arange(DEVICES, dtype=jnp.int32)[:, None]
    target_row = jnp.where(slot_rank < CAP, ids_dev * (DEVICES * CAP) + device_of * CAP + slot_rank, EXPERTS * DEVICES * CAP).reshape(-1).astype(jnp.int32)
    token_of = jnp.arange(TOKENS * TOP, dtype=jnp.int32) // TOP
    source = jnp.full((EXPERTS * DEVICES * CAP,), TOKENS, jnp.int32).at[target_row].set(token_of, mode='drop')
    cos_table, sin_table = rope_tables()

    def forward(params, hidden_in):
        attn_list, experts_all, shared_all, gains_all, router_all = params
        matrices = low(attn_list).reshape(4, HEADS, D, HEAD_DIM)
        w_qkv = jnp.concatenate([matrices[member].transpose(1, 0, 2).reshape(D, D) for member in range(3)], 1)
        w_out = matrices[3].transpose(0, 2, 1).reshape(D, D)
        shared_low = low(shared_all)
        w_sgu = jnp.concatenate([shared_low[0].reshape(D, FFS), shared_low[1].reshape(D, FFS)], 1)
        w_sd = shared_low[2].reshape(FFS, D)

        def one_sequence(seq_pair):
            return mix_sequence(w_qkv, w_out, w_sgu, w_sd, gains_all, cos_table, sin_table, seq_pair[0], seq_pair[1])
        middle, branch_in, shared_out = lax.map(jax.checkpoint(one_sequence), (hidden_in.reshape(SEQS, SEQ_LEN, D), prefix))
        middle = middle.reshape(TOKENS, D)
        branch_in = branch_in.reshape(TOKENS, D)
        shared_out = shared_out.reshape(TOKENS, D)
        logits = low_back(jnp.dot(branch_in, low(router_all), precision=HIGHEST))
        chosen = jnp.take_along_axis(logits, routes, 1)
        exp_chosen = jnp.exp(chosen - lax.optimization_barrier(jnp.max(chosen, -1, keepdims=True)))
        gate_w = exp_chosen / lax.optimization_barrier(jnp.sum(exp_chosen, -1, keepdims=True))
        padded_in = jnp.concatenate([branch_in, jnp.zeros((1, D), branch_in.dtype)], 0)
        rows = low_back(jnp.take(padded_in, source, axis=0)).reshape(EXPERTS, DEVICES * CAP, D)
        expert_low = low(experts_all)
        expert_out = lax.map(jax.checkpoint(expert_block), (rows, expert_low[:, 0].reshape(EXPERTS, D, FF), expert_low[:, 1].reshape(EXPERTS, D, FF), expert_low[:, 2].reshape(EXPERTS, FF, D)))
        padded_out = jnp.concatenate([expert_out.reshape(EXPERTS * DEVICES * CAP, D), jnp.zeros((1, D), expert_out.dtype)], 0)
        picked = jnp.take(padded_out, target_row, axis=0).reshape(TOKENS, TOP, D)
        expert_sum = lax.optimization_barrier(jnp.sum(gate_w[:, :, None] * picked, 1))
        return middle + shared_out + expert_sum
    params = (jnp.take(attn_master, slot_of, axis=0), expert_master, shared_master, norm_gains, router)
    result_out, pullback = jax.vjp(forward, params, tokens_in.astype(jnp.float32))
    grad_params, tokens_grad = pullback(cotangent.astype(jnp.float32))
    grad_attn, grad_expert, grad_shared, grad_gains, grad_router = grad_params
    attn_w, attn_m, attn_n = adam_update(params[0], jnp.take(attn_first, slot_of, axis=0), jnp.take(attn_second, slot_of, axis=0), grad_attn, RATE_ATTENTION, WEIGHT_DECAY)
    attn_new = jnp.zeros_like(attn_master).at[slot_of].set(attn_w)
    attn_first_new = jnp.zeros_like(attn_first).at[slot_of].set(attn_m)
    attn_second_new = jnp.zeros_like(attn_second).at[slot_of].set(attn_n)
    attn_copy = attn_w.astype(jnp.bfloat16)
    expert_new, expert_first_new, expert_second_new = adam_update(expert_master, expert_first, expert_second, grad_expert, RATE_MATRIX, WEIGHT_DECAY)
    shared_new, shared_first_new, shared_second_new = adam_update(shared_master, shared_first, shared_second, grad_shared, RATE_MATRIX, WEIGHT_DECAY)
    gains_new, gains_first_new, gains_second_new = adam_update(norm_gains, gains_first, gains_second, grad_gains, RATE_GAIN, 0.0)
    router_new, router_first_new, router_second_new = adam_update(router, router_first, router_second, grad_router, RATE_ROUTER, WEIGHT_DECAY)
    return (result_out.astype(jnp.bfloat16), tokens_grad, attn_new, attn_first_new, attn_second_new, attn_copy, expert_new, expert_first_new, expert_second_new, shared_new, shared_first_new, shared_second_new, gains_new, gains_first_new, gains_second_new, router_new, router_first_new, router_second_new)
```

```python
import functools
import jax
import jax.numpy as jnp
from jax import lax
from jax.experimental import pallas as pl
from jax.experimental.pallas import tpu as pltpu
from jax.sharding import Mesh, PartitionSpec as P

HEADS = 12
HEAD_DIM = 64
FF = 2048
FFS = 2048
SEQ_LEN = 1024
STEP = 5

NORM_EPSILON = 1e-06
ADAM_EPSILON = 1e-08
FIRST_BETA = 0.5
SECOND_BETA = 0.5
WEIGHT_DECAY = 0.1
RATE_ATTENTION = 0.06
RATE_MATRIX = 0.03
RATE_ROUTER = 0.02
RATE_GAIN = 0.3
ROPE_BASE = 10000.0

PACK = 4
HALF = HEAD_DIM // 2
GROUP = PACK * HEAD_DIM
GROUPS = HEADS // PACK
BLOCK = 256
LONGEST_PREFIX = SEQ_LEN // 2
VMEM_BYTES = 60 * 1024 * 1024
AT_ONCE = pl.CostEstimate(flops=0, bytes_accessed=0, transcendentals=0)
LOW = jnp.bfloat16
WIDE = jnp.float32


def dot_nn(left, right):
    return jnp.dot(left, right, preferred_element_type=WIDE)


def dot_nt(left, right):
    return lax.dot_general(left, right, (((1,), (1,)), ((), ())), preferred_element_type=WIDE)


ANYWHERE = pl.BlockSpec(memory_space=pl.ANY)


def ignoring(kernel, first, count):
    return lambda *refs: kernel(*refs[:first], *refs[first + count :])


def side_by_side(ref):
    return jnp.concatenate([ref[piece] for piece in range(ref.shape[0])], 1)


def whole(shape):
    return pl.BlockSpec(shape, lambda *_: (0,) * len(shape))


def once(shape):
    return pl.BlockSpec(shape, lambda *_: (0,) * len(shape), pipeline_mode=pl.Buffered(1))


def params():
    return pltpu.CompilerParams(vmem_limit_bytes=VMEM_BYTES)


def chunk_of(shape):
    return (lax.broadcasted_iota(jnp.int32, shape, 1) & 127) >> 5


def gather_columns_kernel(slot_ref, slots_ref, out_ref, wide_ref):
    pairs = slots_ref.shape[1]
    chunk = chunk_of((pairs, 128))
    for group in range(GROUPS):
        for kind in range(4):
            parts = [
                slots_ref[slot_ref[kind * HEADS + group * PACK + head]].astype(WIDE)
                for head in range(PACK)
            ]
            for parity in range(2):
                for half in range(2):
                    source = 2 * parity + half
                    packed = None
                    for head in range(PACK):
                        shift = (head - source) * HALF % 128
                        moved = pltpu.roll(parts[head], shift, 1) if shift else parts[head]
                        packed = moved if head == 0 else jnp.where(chunk == head, moved, packed)
                    place = (group * 4 + kind) * 2 + half
                    wide_ref[place, pl.ds(parity, pairs, stride=2), :] = packed
    for place in range(wide_ref.shape[0]):
        out_ref[:, place * 128 : (place + 1) * 128] = wide_ref[place].astype(LOW)


def gather_columns(slots, slot_of):
    pairs = slots.shape[1]
    shape = (2 * pairs, GROUPS * 4 * GROUP)
    return pl.pallas_call(
        gather_columns_kernel,
        out_shape=jax.ShapeDtypeStruct(shape, LOW),
        in_specs=[pl.BlockSpec(memory_space=pltpu.SMEM), pl.BlockSpec(memory_space=pltpu.VMEM)],
        out_specs=pl.BlockSpec(memory_space=pltpu.VMEM),
        scratch_shapes=[pltpu.VMEM((shape[1] // 128, shape[0], 128), WIDE)],
        compiler_params=params(),
    )(slot_of, slots)


def split_columns_kernel(slot_ref, grad_ref, *refs):
    out_refs, slots_ref, wide_ref = refs[:-2], refs[-2], refs[-1]
    slots, pairs, _ = slots_ref.shape
    chunk = chunk_of((pairs, 128))
    slots_ref[...] = jnp.zeros_like(slots_ref)
    for group in range(GROUPS):
        first = group * 4 * GROUP
        for place in range(wide_ref.shape[0]):
            columns = slice(first + place * 128, first + (place + 1) * 128)
            wide_ref[place] = grad_ref[:, columns].astype(WIDE)
        for kind in range(4):
            blocks = [
                wide_ref[kind * 2 + source % 2, pl.ds(source // 2, pairs, stride=2), :]
                for source in range(4)
            ]
            for head in range(PACK):
                packed = None
                for source in range(4):
                    shift = (source - head) * HALF % 128
                    moved = pltpu.roll(blocks[source], shift, 1) if shift else blocks[source]
                    packed = moved if source == 0 else jnp.where(chunk == source, moved, packed)
                slots_ref[slot_ref[kind * HEADS + group * PACK + head]] = packed.astype(LOW)
    held = slots // len(out_refs)
    for index, out_ref in enumerate(out_refs):
        out_ref[...] = slots_ref[index * held : (index + 1) * held]


def split_columns(grad, slot_of, partners, held):
    rows = grad.shape[0]
    shape = (held, rows // 2, 128)
    return pl.pallas_call(
        split_columns_kernel,
        out_shape=[jax.ShapeDtypeStruct(shape, LOW)] * partners,
        in_specs=[pl.BlockSpec(memory_space=pltpu.SMEM), pl.BlockSpec(memory_space=pltpu.VMEM)],
        out_specs=[pl.BlockSpec(memory_space=pltpu.VMEM)] * partners,
        scratch_shapes=[
            pltpu.VMEM((partners * held, rows // 2, 128), LOW),
            pltpu.VMEM((4 * GROUP // 128, rows, 128), WIDE),
        ],
        compiler_params=params(),
    )(slot_of, grad)


def key_extent(block):
    return max((block + 1) * BLOCK, LONGEST_PREFIX)


def attend_forward_kernel(
    prefix_ref, token_ref, gain_ref, cos_ref, sin_ref, w_ref,
    query_ref, key_ref, value_ref, head_ref, total_ref, normed_ref, middle_ref, branch_ref,
    sum_ref,
):
    group = pl.program_id(0)
    length, width = token_ref.shape

    @pl.when(group == 0)
    def _():
        hidden = token_ref[...].astype(WIDE)
        scale = lax.rsqrt(jnp.mean(hidden * hidden, -1, keepdims=True) + NORM_EPSILON)
        normed_ref[...] = (hidden * scale * gain_ref[0:1, :]).astype(LOW)
        middle_ref[...] = hidden
        total_ref[...] = jnp.zeros_like(total_ref)

    projected = dot_nn(normed_ref[...], w_ref[:, : 3 * GROUP])
    cos, sin = cos_ref[...], sin_ref[...]
    for kind, ref in enumerate((query_ref, key_ref)):
        lead = projected[:, kind * GROUP : kind * GROUP + 128]
        tail = projected[:, kind * GROUP + 128 : (kind + 1) * GROUP]
        ref[:, :128] = (lead * cos - tail * sin).astype(LOW)
        ref[:, 128:] = (tail * cos + lead * sin).astype(LOW)
    value_ref[...] = projected[:, 2 * GROUP :].astype(LOW)
    prefix = prefix_ref[0]

    lane = lax.broadcasted_iota(jnp.int32, (1, GROUP), 1)
    total_lane = lax.broadcasted_iota(jnp.int32, (BLOCK, 128), 1)
    owned = [chunk_of((1, GROUP)) == head for head in range(PACK)]
    ones = [lane == (head + 1) % PACK * HALF for head in range(PACK)]
    items = [(head, block) for head in range(PACK) for block in range(length // BLOCK)]

    def score(head, block):
        rows = slice(block * BLOCK, (block + 1) * BLOCK)
        own = owned[head].astype(WIDE).astype(LOW)
        return dot_nt(
            query_ref[rows, :] * (own * HEAD_DIM ** (-0.5)), key_ref[: key_extent(block), :]
        )

    def attend(head, block, scores):
        start = block * BLOCK
        rows = slice(start, start + BLOCK)
        edge = scores[:, start:]
        key_pos = lax.broadcasted_iota(jnp.int32, edge.shape, 1)
        allowed = key_pos <= lax.broadcasted_iota(jnp.int32, edge.shape, 0)
        if start < LONGEST_PREFIX:
            allowed = allowed | (key_pos < prefix - start)
        edge = jnp.where(allowed, edge, -1e30)
        scores = jnp.concatenate([scores[:, :start], edge], 1) if start else edge
        peak = jnp.max(scores, -1, keepdims=True)
        weights = jnp.exp(scores - peak).astype(LOW)
        own = owned[head].astype(WIDE).astype(LOW)
        values = value_ref[: key_extent(block), :] * own + ones[head].astype(WIDE).astype(LOW)
        mixed = dot_nn(weights, values)
        total = jnp.sum(jnp.where(ones[head], mixed, 0.0), -1, keepdims=True)
        mixed = jnp.where(owned[head], mixed * (1.0 / total), 0.0)
        sum_ref[rows, :] = mixed if head == 0 else sum_ref[rows, :] + mixed
        total_ref[rows, :] = jnp.where(
            total_lane == group * PACK + head, peak + jnp.log(total), total_ref[rows, :]
        )

    ahead = score(*items[0])
    for index, item in enumerate(items):
        scores = ahead
        if index + 1 < len(items):
            ahead = score(*items[index + 1])
        attend(*item, scores)
    heads = sum_ref[...].astype(LOW)
    head_ref[...] = heads
    middle_ref[...] += dot_nt(heads, w_ref[:, 3 * GROUP :])

    @pl.when(group == pl.num_programs(0) - 1)
    def _():
        middle = middle_ref[...]
        scale = lax.rsqrt(jnp.mean(middle * middle, -1, keepdims=True) + NORM_EPSILON)
        branch_ref[...] = (middle * scale * gain_ref[1:2, :]).astype(LOW)


def attend_forward(prefix, tokens, gains, cos, sin, w_attn, after):
    length, width = tokens.shape
    low = lambda columns: jax.ShapeDtypeStruct((length, columns), LOW)
    grouped = pl.BlockSpec((length, GROUP), lambda group: (0, group))
    return pl.pallas_call(
        ignoring(attend_forward_kernel, 6, len(after)),
        grid=(GROUPS,),
        out_shape=[
            low(width), low(width), low(width), low(width),
            jax.ShapeDtypeStruct((length, 128), WIDE),
            low(width),
            jax.ShapeDtypeStruct((length, width), WIDE),
            low(width),
        ],
        in_specs=[
            pl.BlockSpec(memory_space=pltpu.SMEM),
            once(tokens.shape),
            once(gains.shape),
            once(cos.shape),
            once(sin.shape),
            pl.BlockSpec((width, 4 * GROUP), lambda group: (0, group)),
        ]
        + [ANYWHERE] * len(after),
        out_specs=[
            grouped, grouped, grouped, grouped,
            whole((length, 128)),
            whole((length, width)),
            whole((length, width)),
            whole((length, width)),
        ],
        scratch_shapes=[pltpu.VMEM((length, GROUP), WIDE)],
        compiler_params=params(),
        cost_estimate=pl.CostEstimate(
            flops=25_000_000_000, bytes_accessed=20_000_000, transcendentals=9_000_000
        ),
    )(prefix, tokens, gains, cos, sin, w_attn, *after)


def attend_backward_kernel(
    prefix_ref, query_ref, key_ref, value_ref, head_ref, total_ref, cos_ref, sin_ref,
    normed_t_ref, grad_ref, grad_t_ref, w_ref, grad_w_ref, grad_normed_ref,
    total_t_ref, scaled_ref, key_t_ref, grad_head_ref, center_ref,
    probs_ref, grad_scores_ref, grad_query_t_ref, grad_key_ref, grad_value_ref,
):
    step = pl.program_id(0)
    length = query_ref.shape[0]

    @pl.when(step == 0)
    def _():
        total_t_ref[...] = total_ref[...].T
        grad_normed_ref[...] = jnp.zeros_like(grad_normed_ref)

    scaled_ref[...] = query_ref[...] * HEAD_DIM ** (-0.5)
    key_t = key_ref[...].T
    for head in range(PACK):
        for half in range(2):
            first = half * 128 + head * HALF
            key_t_ref[head, half * HALF : (half + 1) * HALF, :] = key_t[first : first + HALF]
    grad_heads = dot_nn(grad_ref[...], w_ref[:, 3 * GROUP :]).astype(LOW)
    grad_head_ref[...] = grad_heads
    product = grad_heads.astype(WIDE) * head_ref[...].astype(WIDE)
    leading = product.astype(LOW)
    rest = (product - leading.astype(WIDE)).astype(LOW)
    head_row = lax.broadcasted_iota(jnp.int32, (16, GROUP), 0)
    select = (chunk_of((16, GROUP)) == head_row).astype(WIDE).astype(LOW)
    center_ref[...] = dot_nt(select, leading) + dot_nt(select, rest)
    prefix = prefix_ref[0]
    owned = [(chunk_of((1, GROUP)) == head).astype(WIDE).astype(LOW) for head in range(PACK)]
    items = [(head, block) for head in range(PACK) for block in range(length // BLOCK)]

    def score(head, block):
        rows = slice(block * BLOCK, (block + 1) * BLOCK)
        extent = key_extent(block)
        return (
            dot_nt(key_ref[:extent, :], scaled_ref[rows, :] * owned[head]),
            dot_nt(value_ref[:extent, :], grad_head_ref[rows, :] * owned[head]),
        )

    def weigh(head, block, scores, grad_probs):
        start, extent = block * BLOCK, key_extent(block)
        rows = slice(start, start + BLOCK)
        totals = total_t_ref[pl.ds(step * PACK + head, 1), rows]
        probs = jnp.exp(scores - totals)
        edge = probs[start:, :]
        key_pos = lax.broadcasted_iota(jnp.int32, edge.shape, 0)
        allowed = key_pos <= lax.broadcasted_iota(jnp.int32, edge.shape, 1)
        if start < LONGEST_PREFIX:
            allowed = allowed | (key_pos < prefix - start)
        edge = jnp.where(allowed, edge, 0.0)
        probs = jnp.concatenate([probs[:start, :], edge], 0) if start else edge
        grad_scores = (probs * (grad_probs - center_ref[head : head + 1, rows])).astype(LOW)
        probs_ref[head % 2, :extent, rows] = probs.astype(LOW)
        grad_scores_ref[head % 2, :extent, rows] = grad_scores
        grad_query_t = dot_nn(key_t_ref[head, :, :extent], grad_scores)
        for half in range(2):
            first = half * 128 + head * HALF
            grad_query_t_ref[first : first + HALF, rows] = grad_query_t[
                half * HALF : (half + 1) * HALF
            ]

    def gather_keys(head):
        queries, grads = scaled_ref[...] * owned[head], grad_head_ref[...] * owned[head]
        first = 0
        while first < length:
            seen = 0 if first < LONGEST_PREFIX else first
            keys = slice(first, LONGEST_PREFIX if first < LONGEST_PREFIX else first + BLOCK)
            for ref, source, right in (
                (grad_value_ref, probs_ref, grads),
                (grad_key_ref, grad_scores_ref, queries),
            ):
                part = dot_nn(source[head % 2, keys, seen:], right[seen:, :])
                ref[keys, :] = part if head == 0 else ref[keys, :] + part
            first = keys.stop

    ahead = score(*items[0])
    for index, (head, block) in enumerate(items):
        scores = ahead
        if index + 1 < len(items):
            ahead = score(*items[index + 1])
        weigh(head, block, *scores)
        if (block + 1) * BLOCK == length:
            gather_keys(head)
    cos, sin = cos_ref[...], sin_ref[...]
    pieces = []
    for grad in (grad_query_t_ref[...].T * HEAD_DIM ** (-0.5), grad_key_ref[...]):
        lead, tail = grad[:, :128], grad[:, 128:]
        pieces.append((lead * cos + tail * sin).astype(LOW))
        pieces.append((tail * cos - lead * sin).astype(LOW))
    pieces.append(grad_value_ref[...].astype(LOW))
    grads = jnp.concatenate(pieces, 1)
    grad_w_ref[:, : 3 * GROUP] = dot_nn(side_by_side(normed_t_ref), grads).astype(LOW)
    grad_w_ref[:, 3 * GROUP :] = dot_nn(side_by_side(grad_t_ref), head_ref[...]).astype(LOW)
    grad_normed_ref[...] += dot_nt(grads, w_ref[:, : 3 * GROUP])


def attend_backward(
    prefix, query, key, value, heads, totals, cos, sin, normed_t, grad, grad_t, w_attn
):
    length, width = grad.shape
    grouped = pl.BlockSpec((length, GROUP), lambda step: (0, step))
    return pl.pallas_call(
        attend_backward_kernel,
        grid=(GROUPS,),
        out_shape=[
            jax.ShapeDtypeStruct((width, GROUPS * 4 * GROUP), LOW),
            jax.ShapeDtypeStruct((length, width), WIDE),
        ],
        in_specs=[
            pl.BlockSpec(memory_space=pltpu.SMEM),
            grouped, grouped, grouped, grouped,
            once(totals.shape), once(cos.shape), once(sin.shape), once(normed_t.shape),
            once(grad.shape), once(grad_t.shape),
            pl.BlockSpec((width, 4 * GROUP), lambda step: (0, step)),
        ],
        out_specs=[
            pl.BlockSpec((width, 4 * GROUP), lambda step: (0, step)),
            whole((length, width)),
        ],
        scratch_shapes=[
            pltpu.VMEM((128, length), WIDE),
            pltpu.VMEM((length, GROUP), LOW),
            pltpu.VMEM((PACK, HEAD_DIM, length), LOW),
            pltpu.VMEM((length, GROUP), LOW),
            pltpu.VMEM((16, length), WIDE),
            pltpu.VMEM((2, length, length), LOW),
            pltpu.VMEM((2, length, length), LOW),
            pltpu.VMEM((GROUP, length), WIDE),
            pltpu.VMEM((length, GROUP), WIDE),
            pltpu.VMEM((length, GROUP), WIDE),
        ],
        compiler_params=params(),
        cost_estimate=AT_ONCE,
    )(prefix, query, key, value, heads, totals, cos, sin, normed_t, grad, grad_t, w_attn)


def swiglu_blocks(blocks, rows_of, w_gu_ref, w_d_ref, act_ref, grad_act_ref, sum_ref, grad_sum_ref):
    subs = w_d_ref.shape[0] // HIDDEN_BLOCK
    items = [(block, sub) for block in range(blocks) for sub in range(subs)]

    def into(block, sub):
        _, tokens, grads_in = rows_of(block)
        units = slice(sub * HIDDEN_BLOCK, (sub + 1) * HIDDEN_BLOCK)
        both = slice(2 * sub * HIDDEN_BLOCK, 2 * (sub + 1) * HIDDEN_BLOCK)
        return dot_nn(tokens, w_gu_ref[:, both]), dot_nt(grads_in, w_d_ref[units, :])

    def middle(block, sub, gate_up, grad_hidden):
        rows, _, _ = rows_of(block)
        units = slice(sub * HIDDEN_BLOCK, (sub + 1) * HIDDEN_BLOCK)
        both = slice(2 * sub * HIDDEN_BLOCK, 2 * (sub + 1) * HIDDEN_BLOCK)
        gate, up = gate_up[:, :HIDDEN_BLOCK], gate_up[:, HIDDEN_BLOCK:]
        sig = 0.5 * jnp.tanh(0.5 * gate) + 0.5
        act = gate * sig
        act_ref[rows, units] = (act * up).astype(LOW)
        grad_act_ref[rows, both] = jnp.concatenate(
            [
                (grad_hidden * up * (sig + act * (1.0 - sig))).astype(LOW),
                (grad_hidden * act).astype(LOW),
            ],
            1,
        )

    def out(block):
        rows, _, _ = rows_of(block)
        sum_ref[rows, :] += dot_nn(act_ref[rows, :], w_d_ref[...])
        grad_sum_ref[rows, :] += dot_nt(grad_act_ref[rows, :], w_gu_ref[...])

    ahead = into(*items[0])
    for index, item in enumerate(items):
        products = ahead
        if index + 1 < len(items):
            ahead = into(*items[index + 1])
        middle(*item, *products)
        if item[1] == subs - 1:
            out(item[0])


def swiglu_kernel(parts, rows_ref, grad_ref, rows_t_ref, grad_t_ref, *refs):
    w_gu_refs, w_d_refs, refs = refs[:parts], refs[parts : 2 * parts], refs[2 * parts :]
    out_ref, grad_rows_ref, refs = refs[0], refs[1], refs[2:]
    grad_gu_refs, grad_d_refs = refs[0 : 2 * parts : 2], refs[1 : 2 * parts : 2]
    act_ref, grad_act_ref = refs[2 * parts :]
    step = pl.program_id(0)
    count = rows_ref.shape[0]
    per_part = pl.num_programs(0) // parts

    @pl.when(step == 0)
    def _():
        out_ref[...] = jnp.zeros_like(out_ref)
        grad_rows_ref[...] = jnp.zeros_like(grad_rows_ref)

    def one_part(w_gu_ref, w_d_ref, grad_gu_ref, grad_d_ref):
        def rows_of(block):
            rows = slice(block * ROW_BLOCK, (block + 1) * ROW_BLOCK)
            return rows, rows_ref[rows, :], grad_ref[rows, :]

        swiglu_blocks(
            count // ROW_BLOCK, rows_of, w_gu_ref, w_d_ref, act_ref, grad_act_ref, out_ref,
            grad_rows_ref,
        )
        grad_gu_ref[...] = dot_nn(side_by_side(rows_t_ref), grad_act_ref[...]).astype(LOW)
        grad_d_ref[...] = dot_nn(side_by_side(grad_t_ref), act_ref[...]).astype(LOW).T

    for part in range(parts):
        pl.when(step // per_part == part)(
            functools.partial(
                one_part, w_gu_refs[part], w_d_refs[part], grad_gu_refs[part], grad_d_refs[part]
            )
        )


ROW_BLOCK = 1024
HIDDEN_BLOCK = 256


def swiglu(rows, grad, rows_t, grad_t, w_gu, w_d):
    count, width = rows.shape
    parts = len(w_d)
    hidden = w_d[0].shape[0]
    chunk = EXPERT_BLOCK
    per_part = hidden // chunk

    def place(part):
        return lambda step: jnp.clip(step - part * per_part, 0, per_part - 1)

    gu_specs = [
        pl.BlockSpec((width, 2 * chunk), lambda step, at=place(part): (0, at(step)))
        for part in range(parts)
    ]
    d_specs = [
        pl.BlockSpec((chunk, width), lambda step, at=place(part): (at(step), 0))
        for part in range(parts)
    ]
    gu_shape = jax.ShapeDtypeStruct((width, 2 * hidden), LOW)
    d_shape = jax.ShapeDtypeStruct((hidden, width), LOW)
    total = parts * hidden
    return pl.pallas_call(
        functools.partial(swiglu_kernel, parts),
        grid=(parts * per_part,),
        out_shape=[jax.ShapeDtypeStruct((count, width), WIDE)] * 2 + [gu_shape, d_shape] * parts,
        in_specs=[once(each.shape) for each in (rows, grad, rows_t, grad_t)] + gu_specs + d_specs,
        out_specs=[whole((count, width))] * 2
        + [spec for pair in zip(gu_specs, d_specs) for spec in pair],
        scratch_shapes=[
            pltpu.VMEM((count, chunk), LOW),
            pltpu.VMEM((count, 2 * chunk), LOW),
        ],
        compiler_params=params(),
        cost_estimate=pl.CostEstimate(
            flops=18 * count * width * total,
            bytes_accessed=12 * width * total + 12 * count * width,
            transcendentals=count * total,
        ),
    )(rows, grad, rows_t, grad_t, *w_gu, *w_d)


def wait_all(values, *others):
    count = len(values)
    anywhere = pl.BlockSpec(memory_space=pl.ANY)
    return pl.pallas_call(
        lambda *refs: None,
        out_shape=[jax.ShapeDtypeStruct(value.shape, value.dtype) for value in values],
        in_specs=[anywhere] * (count + len(others)),
        out_specs=[anywhere] * count,
        input_output_aliases={index: index for index in range(count)},
        cost_estimate=AT_ONCE,
    )(*values, *others)


def wait_for(value, *others):
    return wait_all([value], *others)[0]


def pair_gates(chosen):
    peak = functools.reduce(jnp.maximum, chosen)
    weights = [jnp.exp(each - peak) for each in chosen]
    total = sum(weights[1:], weights[0])
    return [each / total for each in weights]


def dispatch_kernel(
    here_ref, route_ref, target_ref, branch_ref, grad_ref, router_ref, *refs
):
    partner = pl.program_id(0)
    partners = (len(refs) - 3) // 2
    turned_refs, gate_ref = refs[-3:-1], refs[-1]
    top, count = route_ref.shape
    half = refs[0].shape[1]
    capacity = 2 * half

    @pl.when(partner == 0)
    def _():
        logits = dot_nt(router_ref[...], branch_ref[...])
        row = lax.broadcasted_iota(jnp.int32, logits.shape, 0)
        chosen = [
            jnp.sum(jnp.where(row == route_ref[pick : pick + 1, :], logits, 0.0), 0, keepdims=True)
            for pick in range(top)
        ]
        for pick, gate in enumerate(pair_gates(chosen)):
            gate_ref[pick : pick + 1, :] = gate

    piece = pl.ds(pl.multiple_of(jnp.minimum(partner, count // BLOCK - 1) * BLOCK, BLOCK), BLOCK)
    for source_ref, turned_ref in zip((branch_ref, grad_ref), turned_refs):
        turned_ref[0] = source_ref[piece, :].T
    expert = here_ref[0] ^ partner
    place = expert * capacity + lax.broadcasted_iota(jnp.int32, (capacity, count), 0)
    spread = jnp.zeros((capacity, count), WIDE)
    gates = jnp.zeros((capacity, count), WIDE)
    for pick in range(top):
        here = target_ref[pick : pick + 1, :] == place
        spread = jnp.where(here, 1.0, spread)
        gates = jnp.where(here, gate_ref[pick : pick + 1, :], gates)
    spread = spread.astype(LOW)
    rows = dot_nn(spread, branch_ref[...]).astype(LOW)
    grads = dot_nn(spread, grad_ref[...])
    grads = (grads * jnp.sum(gates, 1, keepdims=True)).astype(LOW)

    def store(first_ref, second_ref):
        for ref, part in ((first_ref, slice(0, half)), (second_ref, slice(half, capacity))):
            ref[0] = rows[part]
            ref[1] = grads[part]

    for index in range(partners):
        pl.when(partner == index)(
            functools.partial(store, refs[index], refs[partners + index])
        )


def dispatch(here, routes_t, target_t, branch_in, grad, router_t, partners, capacity):
    count, width = branch_in.shape
    top = routes_t.shape[0]
    shape = (2, capacity // 2, width)
    outs = pl.pallas_call(
        dispatch_kernel,
        grid=(partners,),
        out_shape=[jax.ShapeDtypeStruct(shape, LOW)] * (2 * partners)
        + [jax.ShapeDtypeStruct((count // BLOCK, width, BLOCK), LOW)] * 2
        + [jax.ShapeDtypeStruct((top, count), WIDE)],
        in_specs=[
            pl.BlockSpec(memory_space=pltpu.SMEM),
            once(routes_t.shape), once(target_t.shape), once(branch_in.shape), once(grad.shape),
            once(router_t.shape),
        ],
        out_specs=[whole(shape)] * (2 * partners)
        + [
            pl.BlockSpec(
                (1, width, BLOCK), lambda step: (jnp.minimum(step, count // BLOCK - 1), 0, 0)
            )
        ]
        * 2
        + [whole((top, count))],
        compiler_params=params(),
        cost_estimate=pl.CostEstimate(
            flops=4 * partners * capacity * count * width,
            bytes_accessed=4 * (partners * capacity + count) * width,
            transcendentals=0,
        ),
    )(here, routes_t, target_t, branch_in, grad, router_t)
    return outs[:partners], outs[partners : 2 * partners], *outs[2 * partners : -1]


def expert_kernel(sources, *refs):
    rows_refs, refs = refs[:sources], refs[sources:]
    gu_stack_ref, d_stack_ref, refs = refs[0], refs[1], refs[2:]
    out_refs, refs = refs[:sources], refs[sources:]
    act_ref, grad_act_ref, turned_ref, out_sum_ref, grad_sum_ref, w_gu_ref, w_d_ref = refs
    step = pl.program_id(0)
    _, per_source, width = rows_refs[0].shape
    block = max(1, ROW_BLOCK // per_source)
    count = block * per_source

    @pl.when(step == 0)
    def _():
        out_sum_ref[...] = jnp.zeros_like(out_sum_ref)
        grad_sum_ref[...] = jnp.zeros_like(grad_sum_ref)

    for stack_ref, w_ref in ((gu_stack_ref, w_gu_ref), (d_stack_ref, w_d_ref)):
        columns = w_ref.shape[1] // 256
        tall = stack_ref.shape[1] // columns
        for column in range(columns):
            w_ref[:, column * 256 : (column + 1) * 256] = stack_ref[
                :, column * tall : (column + 1) * tall, :
            ].reshape(w_ref.shape[0], 256)

    def gather(index, member):
        return jnp.concatenate(
            [ref[member] for ref in rows_refs[index * block : (index + 1) * block]], 0
        )

    def rows_of(index):
        return slice(index * count, (index + 1) * count), gather(index, 0), gather(index, 1)

    swiglu_blocks(
        sources // block, rows_of, w_gu_ref, w_d_ref, act_ref, grad_act_ref, out_sum_ref,
        grad_sum_ref,
    )
    for piece in range(2 * (sources // block)):

        @pl.when(step == piece)
        def _():
            turned_ref[0, 0] = gather(piece % (sources // block), piece // (sources // block)).T

    @pl.when(step == pl.num_programs(0) - 1)
    def _():
        for index, ref in enumerate(out_refs):
            rows = slice(index * per_source, (index + 1) * per_source)
            ref[0] = out_sum_ref[rows, :].astype(LOW)
            ref[1] = grad_sum_ref[rows, :].astype(LOW)


EXPERT_BLOCK = 512


def expert_pass(rows, stack, after):
    sources = len(rows)
    _, per_source, width = rows[0].shape
    count = sources * per_source
    devices = stack.shape[0]
    chunk = EXPERT_BLOCK
    hidden = FF
    steps = hidden // chunk
    gu_tall = 2 * chunk // 256 * (width // devices)
    d_tall = width // 256 * (hidden // devices)
    blocks = 2 * count // ROW_BLOCK
    assert steps >= blocks and gu_tall * steps % d_tall == 0
    outs = pl.pallas_call(
        ignoring(functools.partial(expert_kernel, sources), sources + 2, len(after)),
        grid=(steps,),
        out_shape=[jax.ShapeDtypeStruct(rows[0].shape, LOW)] * sources
        + [
            jax.ShapeDtypeStruct((count, hidden), LOW),
            jax.ShapeDtypeStruct((count, 2 * hidden), LOW),
            jax.ShapeDtypeStruct((2, blocks // 2, width, ROW_BLOCK), LOW),
        ],
        in_specs=[once(rows[0].shape)] * sources
        + [
            pl.BlockSpec((devices, gu_tall, 256), lambda step: (0, step, 0)),
            pl.BlockSpec(
                (chunk * devices // hidden, d_tall, 256),
                lambda step: (step, gu_tall * steps // d_tall, 0),
            ),
        ]
        + [ANYWHERE] * len(after),
        out_specs=[whole(rows[0].shape)] * sources
        + [
            pl.BlockSpec((count, chunk), lambda step: (0, step)),
            pl.BlockSpec((count, 2 * chunk), lambda step: (0, step)),
            pl.BlockSpec(
                (1, 1, width, ROW_BLOCK),
                lambda step: (
                    jnp.minimum(step, blocks - 1) // (blocks // 2),
                    jnp.minimum(step, blocks - 1) % (blocks // 2),
                    0,
                    0,
                ),
            ),
        ],
        scratch_shapes=[
            pltpu.VMEM((count, width), WIDE),
            pltpu.VMEM((count, width), WIDE),
            pltpu.VMEM((width, 2 * chunk), LOW),
            pltpu.VMEM((chunk, width), LOW),
        ],
        compiler_params=params(),
        cost_estimate=pl.CostEstimate(
            flops=count * width * hidden, bytes_accessed=width * hidden, transcendentals=0
        ),
    )(*rows, stack, stack, *after)
    return outs[:sources], *outs[sources:]


def weight_grad_kernel(halves, turned, *refs):
    row_refs, act_refs, out_ref = refs[:halves], refs[halves : 2 * halves], refs[-1]
    rows_t = jnp.concatenate([side_by_side(ref.at[0]) for ref in row_refs], 1)
    grad = dot_nn(rows_t, jnp.concatenate([ref[...] for ref in act_refs], 0)).astype(LOW)
    out_ref[...] = grad.T if turned else grad


def weight_grad(rows, acts, member, turned, chunk, after):
    halves = len(acts)
    _, blocks, width, _ = rows[0].shape
    count, units = acts[0].shape
    member_spec = pl.BlockSpec(
        (1, blocks, width, ROW_BLOCK),
        lambda step: (member, 0, 0, 0),
        pipeline_mode=pl.Buffered(1),
    )
    return pl.pallas_call(
        ignoring(
            functools.partial(weight_grad_kernel, halves, turned), 2 * halves, len(after)
        ),
        grid=(units // chunk,),
        out_shape=jax.ShapeDtypeStruct((units, width) if turned else (width, units), LOW),
        in_specs=[member_spec] * halves
        + [pl.BlockSpec((count, chunk), lambda step: (0, step))] * halves
        + [ANYWHERE] * len(after),
        out_specs=pl.BlockSpec((chunk, width), lambda step: (step, 0))
        if turned
        else pl.BlockSpec((width, chunk), lambda step: (0, step)),
        compiler_params=params(),
        cost_estimate=pl.CostEstimate(
            flops=count * width * units // 8, bytes_accessed=width * units // 2, transcendentals=0
        ),
    )(*rows, *acts, *after)


def combine_kernel(
    partners, here_ref, route_ref, target_ref, middle_ref, shared_ref, grad_shared_ref,
    cotangent_ref, branch_ref, normed_ref, gain_ref, router_ref, *refs
):
    halves, refs = (refs[:partners], refs[partners : 2 * partners]), refs[2 * partners :]
    out_ref, grad_ref, grad_low_ref, grad_t_ref, normed_t_ref, grad_router_ref, grad_gain_ref = refs
    normed_t_ref[0] = normed_ref[...].T
    block, top = target_ref.shape
    _, half, width = halves[0][0].shape

    @pl.when(pl.program_id(0) == 0)
    def _():
        grad_router_ref[...] = jnp.zeros_like(grad_router_ref)
        grad_gain_ref[...] = jnp.zeros_like(grad_gain_ref)

    branch = branch_ref[...]
    logits = dot_nt(branch, router_ref[...])
    lane = lax.broadcasted_iota(jnp.int32, logits.shape, 1)
    picked_lane = [lane == route_ref[:, pick : pick + 1] for pick in range(top)]
    gates = pair_gates(
        [jnp.sum(jnp.where(here, logits, 0.0), 1, keepdims=True) for here in picked_lane]
    )
    slot = lax.broadcasted_iota(jnp.int32, (1, partners * half), 1)
    slot = ((slot // half) ^ here_ref[0]) * (2 * half) + slot % half
    picked, grad_rows = 0.0, 0.0
    for index, part in enumerate(halves):
        spread = [
            (target_ref[:, pick : pick + 1] == slot + index * half).astype(WIDE)
            for pick in range(top)
        ]
        stacked = jnp.concatenate(spread, 0).astype(LOW)
        outs, grads = (jnp.concatenate([ref[member] for ref in part], 0) for member in range(2))
        picked = picked + dot_nn(stacked, outs)
        grad_rows = grad_rows + dot_nn(sum(spread[1:], spread[0]).astype(LOW), grads)
    picked = [picked[pick * block : (pick + 1) * block] for pick in range(top)]
    middle = middle_ref[...]
    mixed = sum(gate * rows for gate, rows in zip(gates, picked))
    out_ref[...] = (middle + shared_ref[...] + mixed).astype(LOW)
    cotangent = cotangent_ref[...].astype(WIDE)
    grad_gates = [jnp.sum(cotangent * rows, 1, keepdims=True) for rows in picked]
    mean = sum(gate * grad for gate, grad in zip(gates, grad_gates))
    grad_logits = sum(
        jnp.where(here, gate * (grad - mean), 0.0)
        for here, gate, grad in zip(picked_lane, gates, grad_gates)
    ).astype(LOW)
    grad_router_ref[...] += lax.dot_general(
        grad_logits, branch, (((0,), (0,)), ((), ())), preferred_element_type=WIDE
    )
    grad_branch = grad_shared_ref[...] + dot_nn(grad_logits, router_ref[...]) + grad_rows
    scale = lax.rsqrt(jnp.mean(middle * middle, -1, keepdims=True) + NORM_EPSILON)
    hat = middle * scale
    grad_gain_ref[...] += jnp.sum((grad_branch * hat).reshape(block // 8, 8, width), 0)
    grad_hat = grad_branch * gain_ref[1:2, :]
    grad = cotangent + scale * (grad_hat - hat * jnp.mean(grad_hat * hat, -1, keepdims=True))
    grad_ref[...] = grad
    grad_low_ref[...] = grad.astype(LOW)
    grad_t_ref[0] = grad.astype(LOW).T


def combine(
    here, routes, target, first, second, middle, shared_out, grad_shared, cotangent, branch_in,
    normed, gains, router_t, after
):
    count, width = middle.shape
    top = routes.shape[1]
    lanes = router_t.shape[0]
    partners = len(first)
    rows = pl.BlockSpec((BLOCK, width), lambda step: (step, 0))
    pairs = pl.BlockSpec((BLOCK, top), lambda step: (step, 0))
    return pl.pallas_call(
        ignoring(
            functools.partial(combine_kernel, partners), 11 + 2 * partners, len(after)
        ),
        grid=(count // BLOCK,),
        out_shape=[
            jax.ShapeDtypeStruct((count, width), LOW),
            jax.ShapeDtypeStruct((count, width), WIDE),
            jax.ShapeDtypeStruct((count, width), LOW),
            jax.ShapeDtypeStruct((count // BLOCK, width, BLOCK), LOW),
            jax.ShapeDtypeStruct((count // BLOCK, width, BLOCK), LOW),
            jax.ShapeDtypeStruct((lanes, width), WIDE),
            jax.ShapeDtypeStruct((8, width), WIDE),
        ],
        in_specs=[
            pl.BlockSpec(memory_space=pltpu.SMEM),
            pairs, pairs, rows, rows, rows, rows, rows, rows,
            once(gains.shape), once(router_t.shape),
        ]
        + [once(first[0].shape)] * (2 * partners)
        + [ANYWHERE] * len(after),
        out_specs=[
            rows, rows, rows,
            pl.BlockSpec((1, width, BLOCK), lambda step: (step, 0, 0)),
            pl.BlockSpec((1, width, BLOCK), lambda step: (step, 0, 0)),
            whole((lanes, width)), whole((8, width)),
        ],
        compiler_params=params(),
        cost_estimate=pl.CostEstimate(
            flops=400_000_000_000, bytes_accessed=25_000_000, transcendentals=0
        ),
    )(
        here, routes, target, middle, shared_out, grad_shared, cotangent, branch_in, normed,
        gains, router_t, *first, *second, *after
    )


def swiglu_stacks_kernel(
    partners, rings, col_rows, piece, here_ref, rows_ref, grad_ref, rows_t_ref, grad_t_ref, *refs
):
    stacks, refs = refs[: 4 * partners], refs[4 * partners :]
    out_ref, grad_rows_ref, refs = refs[0], refs[1], refs[2:]
    grad_gu_refs, grad_d_refs, refs = refs[0:4:2], refs[1:4:2], refs[4:]
    w_gu_ref, w_d_ref, act_ref, grad_act_ref = refs
    step = pl.program_id(0)
    count = rows_ref.shape[0]
    per_part = pl.num_programs(0) // 2
    device_cols, device_rows = rings * col_rows, rings * piece
    together = w_d_ref.shape[0] // device_rows

    @pl.when(step == 0)
    def _():
        out_ref[...] = jnp.zeros_like(out_ref)
        grad_rows_ref[...] = jnp.zeros_like(grad_rows_ref)

    def place(gu_ref, d_ref, device):
        for ring in range(rings):
            first = pl.multiple_of(device * device_cols + ring * col_rows, 16)
            for column in range(w_gu_ref.shape[1] // 256):
                w_gu_ref[pl.ds(first, col_rows), column * 256 : (column + 1) * 256] = gu_ref[
                    ring, column * col_rows : (column + 1) * col_rows, :
                ]

        @pl.when(device // together == step % per_part)
        def _():
            for ring in range(rings):
                first = pl.multiple_of(device % together * device_rows + ring * piece, 16)
                for column in range(w_d_ref.shape[1] // 256):
                    w_d_ref[pl.ds(first, piece), column * 256 : (column + 1) * 256] = d_ref[
                        ring, column * piece : (column + 1) * piece, :
                    ]

    for part in range(2):

        @pl.when(step // per_part == part)
        def _():
            for index in range(partners):
                at = 2 * (part * partners + index)
                place(stacks[at], stacks[at + 1], here_ref[0] ^ index)

    def rows_of(block):
        rows = slice(block * ROW_BLOCK, (block + 1) * ROW_BLOCK)
        return rows, rows_ref[rows, :], grad_ref[rows, :]

    swiglu_blocks(
        count // ROW_BLOCK, rows_of, w_gu_ref, w_d_ref, act_ref, grad_act_ref, out_ref,
        grad_rows_ref,
    )
    grad_gu = dot_nn(side_by_side(rows_t_ref), grad_act_ref[...]).astype(LOW)
    grad_d = dot_nn(side_by_side(grad_t_ref), act_ref[...]).astype(LOW).T
    for part in range(2):

        @pl.when(step // per_part == part)
        def _():
            grad_gu_refs[part][...] = grad_gu
            grad_d_refs[part][...] = grad_d


def swiglu_stacks(
    here, rows, grad, rows_t, grad_t, near, far, rings, col_rows, piece, after
):
    count, width = rows.shape
    partners = len(near)
    chunk = EXPERT_BLOCK
    hidden = partners * rings * piece
    per_part = hidden // chunk
    gu_tall, d_tall = 2 * chunk // 256 * col_rows, width // 256 * piece
    assert gu_tall * per_part % d_tall == 0

    def place(part):
        return lambda step: jnp.clip(step - part * per_part, 0, per_part - 1)

    operands, stack_specs, out_specs = [], [], []
    for part, stacks in enumerate((near, far)):
        for stack in stacks:
            operands += [stack.reshape(rings, -1, 256)] * 2
            stack_specs += [
                pl.BlockSpec(
                    (rings, gu_tall, 256), lambda step, at=place(part): (0, at(step), 0)
                ),
                pl.BlockSpec(
                    (rings, d_tall, 256),
                    lambda step: (0, gu_tall * per_part // d_tall, 0),
                    pipeline_mode=pl.Buffered(1),
                ),
            ]
        out_specs += [
            pl.BlockSpec((width, 2 * chunk), lambda step, at=place(part): (0, at(step))),
            pl.BlockSpec((chunk, width), lambda step, at=place(part): (at(step), 0)),
        ]
    kernel = functools.partial(swiglu_stacks_kernel, partners, rings, col_rows, piece)
    return pl.pallas_call(
        ignoring(kernel, 5 + 4 * partners, len(after)),
        grid=(2 * per_part,),
        out_shape=[jax.ShapeDtypeStruct((count, width), WIDE)] * 2
        + [
            jax.ShapeDtypeStruct((width, 2 * hidden), LOW),
            jax.ShapeDtypeStruct((hidden, width), LOW),
        ]
        * 2,
        in_specs=[pl.BlockSpec(memory_space=pltpu.SMEM)]
        + [once(each.shape) for each in (rows, grad, rows_t, grad_t)]
        + stack_specs
        + [ANYWHERE] * len(after),
        out_specs=[whole((count, width))] * 2 + out_specs,
        scratch_shapes=[
            pltpu.VMEM((width, 2 * chunk), LOW),
            pltpu.VMEM((chunk, width), LOW),
            pltpu.VMEM((count, chunk), LOW),
            pltpu.VMEM((count, 2 * chunk), LOW),
        ],
        compiler_params=params(),
        cost_estimate=pl.CostEstimate(
            flops=36 * count * width * hidden,
            bytes_accessed=24 * width * hidden + 12 * count * width,
            transcendentals=2 * count * hidden,
        ),
    )(here, rows, grad, rows_t, grad_t, *operands, *after)


def pack_grads_kernel(rings, col_rows, piece, here_ref, *refs):
    grad_refs, out_refs = refs[:4], refs[4:]

    def place(out_ref):
        for ring in range(rings):
            first = 0
            for near, far, rows in ((*grad_refs[:2], col_rows), (*grad_refs[2:], piece)):
                for column in range(near.shape[1] // 256):
                    part = (
                        slice(ring * rows, (ring + 1) * rows),
                        slice(column * 256, (column + 1) * 256),
                    )
                    out_ref[ring, first : first + rows, :] = (
                        near[part].astype(WIDE) + far[part].astype(WIDE)
                    ).astype(LOW)
                    first += rows

    for index, out_ref in enumerate(out_refs):
        pl.when(pl.program_id(0) == index)(functools.partial(place, out_ref))


def pack_grads(here, partners, near, far, rings, col_rows, piece):
    grads = [near[0], far[0], near[1], far[1]]
    specs = [
        pl.BlockSpec(
            (grad.shape[0] // partners, grad.shape[1]), lambda step, here: (here[0] ^ step, 0)
        )
        for grad in grads
    ]
    rows = sum(grad.shape[0] // partners * grad.shape[1] for grad in grads[::2]) // (256 * rings)
    shape = (rings, rows, 256)
    outs = pl.pallas_call(
        functools.partial(pack_grads_kernel, rings, col_rows, piece),
        grid_spec=pltpu.PrefetchScalarGridSpec(
            num_scalar_prefetch=1,
            grid=(partners,),
            in_specs=specs,
            out_specs=[whole(shape)] * partners,
        ),
        out_shape=[jax.ShapeDtypeStruct(shape, LOW)] * partners,
        compiler_params=params(),
        cost_estimate=pl.CostEstimate(flops=0, bytes_accessed=20_000_000, transcendentals=0),
    )(here, *grads)
    return [out.reshape(rings * rows, 256) for out in outs]


def adam_update(weight, first_state, second_state, gradient, step_rate, decay_rate):
    first_new = FIRST_BETA * first_state + (1.0 - FIRST_BETA) * gradient
    second_new = SECOND_BETA * second_state + (1.0 - SECOND_BETA) * gradient * gradient
    first_hat = first_new / (1.0 - FIRST_BETA**STEP)
    second_hat = second_new / (1.0 - SECOND_BETA**STEP)
    weight_new = weight - step_rate * (
        first_hat / (jnp.sqrt(second_hat) + ADAM_EPSILON) + decay_rate * weight
    )
    return (weight_new, first_new, second_new)


def update_kind(state_refs, new_refs, gradient):
    updated = adam_update(*(ref[0] for ref in state_refs), gradient, RATE_MATRIX, WEIGHT_DECAY)
    for ref, value in zip(new_refs, updated):
        ref[0] = value


def expert_update_kernel(gu_ref, down_ref, *refs):
    state_refs, new_refs, rows_ref = refs[:3], refs[3:6], refs[6]

    def one_kind(kind):
        grad_ref = gu_ref if kind < 2 else down_ref
        columns = state_refs[0].shape[1] // grad_ref.shape[0]
        for column in range(columns):
            left = column * 128
            if kind < 2:
                left = (column // 2 * 2 + kind) * 256 + column % 2 * 128
            rows_ref[pl.ds(column, grad_ref.shape[0], stride=columns), :] = grad_ref[
                :, left : left + 128
            ].astype(WIDE)
        update_kind(state_refs, new_refs, rows_ref[...])

    for kind in range(3):
        pl.when(pl.program_id(0) == kind)(functools.partial(one_kind, kind))


def shared_update_kernel(own_rows, piece, grad_ref, *refs):
    state_refs, new_refs, wide_ref, rows_ref = refs[:3], refs[3:6], refs[6], refs[7]
    blocks = FFS // 256

    def gate_or_up(kind):
        columns = FFS // 128
        lane = lax.broadcasted_iota(jnp.int32, (own_rows, 128), 1)
        for column in range(columns):
            unit = column * piece
            left = unit % 256 // 128 * 128
            low, high = (
                wide_ref[pl.ds((half * blocks + unit // 256 * 2 + kind) * own_rows, own_rows),
                         left : left + 128]
                for half in range(2)
            )
            if unit % 128:
                low = pltpu.roll(low, 64, 1)
            else:
                high = pltpu.roll(high, 64, 1)
            rows_ref[pl.ds(column, own_rows, stride=columns), :] = jnp.where(
                lane < piece, low, high
            )

    def down():
        columns = HEADS * HEAD_DIM // 128
        for column in range(columns):
            first = 2 * blocks * own_rows + column // 2 * piece
            left = column % 2 * 128
            rows_ref[pl.ds(column, piece, stride=columns), :] = wide_ref[
                first : first + piece, left : left + 128
            ]

    @pl.when(pl.program_id(0) == 0)
    def _():
        wide_ref[...] = grad_ref[...].astype(WIDE)

    for kind, place in enumerate(
        (functools.partial(gate_or_up, 0), functools.partial(gate_or_up, 1), down)
    ):

        @pl.when(pl.program_id(0) == kind)
        def _():
            place()
            update_kind(state_refs, new_refs, rows_ref[...])


def update(kernel, grads, states, scratch):
    kinds, rows, _ = states[0].shape
    block = pl.BlockSpec((1, rows, 128), lambda kind: (kind, 0, 0))
    return pl.pallas_call(
        kernel,
        grid=(kinds,),
        out_shape=[jax.ShapeDtypeStruct(states[0].shape, WIDE)] * 3,
        in_specs=[once(grad.shape) for grad in grads] + [block] * 3,
        out_specs=[block] * 3,
        scratch_shapes=scratch + [pltpu.VMEM((rows, 128), WIDE)],
        compiler_params=params(),
        cost_estimate=AT_ONCE,
    )(*grads, *states)


def expert_update(gu, down, states):
    return update(expert_update_kernel, [gu, down], states, [])


def shared_update(grad, own_rows, piece, states):
    kernel = functools.partial(shared_update_kernel, own_rows, piece)
    return update(kernel, [grad], states, [pltpu.VMEM(grad.shape, WIDE)])


def slot_place(owners, own_count, owner_count):
    onehot = (owners[:, None] == jnp.arange(owner_count, dtype=jnp.int32)[None, :]).astype(
        jnp.int32
    )
    prior_count = jnp.sum((jnp.cumsum(onehot, 0) - onehot) * onehot, 1)
    return owners * own_count + prior_count


def rope_tables(length):
    inv_freq = ROPE_BASE ** (-(jnp.arange(HALF, dtype=WIDE) * 2.0 / HEAD_DIM))
    phase_angle = jnp.arange(length, dtype=WIDE)[:, None] * inv_freq[None, :]
    return (jnp.tile(jnp.cos(phase_angle), (1, PACK)), jnp.tile(jnp.sin(phase_angle), (1, PACK)))


def rms_scale(values):
    return lax.rsqrt(jnp.mean(values * values, -1, keepdims=True) + NORM_EPSILON)


def norm_back(grad_normed, hat_values, rms_values, gain):
    grad_hat = grad_normed * gain
    return rms_values * (grad_hat - hat_values * jnp.mean(grad_hat * hat_values, -1, keepdims=True))


SHARD = ("ring", "core")
EVERY = ("expert", "ring", "core")


def to_partner(value, axis, distance):
    size = lax.axis_size(axis)
    return lax.ppermute(value, axis, [(index, index ^ distance) for index in range(size)])


def exchange(values, axis):
    return [values[0]] + [
        to_partner(value, axis, distance) for distance, value in enumerate(values) if distance
    ]


def collect(value, axis):
    return exchange([value] * lax.axis_size(axis), axis)


def add_up(value, axes):
    for axis in axes:
        distance = 1
        while distance < lax.axis_size(axis):
            value = value + to_partner(value, axis, distance)
            distance *= 2
    return value


def gather_rows(part, axes):
    return lax.all_gather(part, axes, axis=0, tiled=True)


def scatter_rows(grad, axes):
    return lax.psum_scatter(grad, axes, scatter_dimension=0, tiled=True)


def to_sibling(value):
    return to_partner(value, "core", 1)


def sum_low(parts):
    return sum((part.astype(WIDE) for part in parts[1:]), parts[0].astype(WIDE)).astype(LOW)


def interleave(gate, up):
    rows, hidden = gate.shape
    blocks = (rows, hidden // HIDDEN_BLOCK, HIDDEN_BLOCK)
    return jnp.concatenate([gate.reshape(blocks), up.reshape(blocks)], 2).reshape(rows, 2 * hidden)


def deinterleave(both):
    rows, columns = both.shape
    blocks = both.reshape(rows, columns // (2 * HIDDEN_BLOCK), 2 * HIDDEN_BLOCK)
    return (
        blocks[:, :, :HIDDEN_BLOCK].reshape(rows, columns // 2),
        blocks[:, :, HIDDEN_BLOCK:].reshape(rows, columns // 2),
    )


def by_core(columns, piece):
    rows, hidden = columns.shape
    return (
        columns.reshape(rows, hidden // (2 * piece), 2, piece)
        .transpose(0, 2, 1, 3)
        .reshape(rows, 2, hidden // 2)
    )


def from_core(columns, piece):
    rows, _, half = columns.shape
    return (
        columns.reshape(rows, 2, half // piece, piece).transpose(0, 2, 1, 3).reshape(rows, 2 * half)
    )


def pack(columns, rows):
    return jnp.concatenate(
        [
            part.reshape(part.shape[0], -1, 256).transpose(1, 0, 2).reshape(-1, 256)
            for part in (columns, rows)
        ],
        0,
    )


def unpack(stack, col_rows, piece):
    per_device = FFS // 256 * col_rows
    stack = stack.reshape(-1, per_device + piece * HEADS * HEAD_DIM // 256, 256)
    devices = stack.shape[0]
    return [
        part.reshape(devices, -1, rows, 256)
        .transpose(0, 2, 1, 3)
        .reshape(devices * rows, -1)
        for part, rows in ((stack[:, :per_device], col_rows), (stack[:, per_device:], piece))
    ]


def body(
    tokens_in,
    cotangent,
    routes,
    prefix,
    owners,
    attn_master,
    attn_first,
    attn_second,
    expert_master,
    expert_first,
    expert_second,
    shared_master,
    shared_first,
    shared_second,
    norm_gains,
    gains_first,
    gains_second,
    router,
    router_first,
    router_second,
):
    tok_count, model_width = tokens_in.shape
    owner_count = lax.axis_size("expert")
    own_count = attn_master.shape[0]
    experts_all = router.shape[1]
    top_count = routes.shape[1]
    capacity = tok_count * top_count // experts_all

    here = lax.axis_index("expert")
    here_ref = here.astype(jnp.int32)[None]
    core = lax.axis_index("core")
    rings = lax.axis_size("ring")
    slot_of = slot_place(owners, own_count, owner_count)
    slot_of = (slot_of // own_count ^ here) * own_count + slot_of % own_count
    attn_cols = gather_columns(
        jnp.concatenate(collect(attn_master.astype(LOW), "expert"), 0), slot_of
    )
    w_attn = gather_rows(attn_cols, SHARD)
    expert_columns = interleave(
        expert_master[0, 0].reshape(-1, FF).astype(LOW),
        expert_master[0, 1].reshape(-1, FF).astype(LOW),
    )
    expert_rows = expert_master[0, 2].reshape(-1, model_width).astype(LOW)
    expert_stack = gather_rows(pack(expert_columns, expert_rows)[None], SHARD)
    shared_down = shared_master[2].reshape(-1, model_width).astype(LOW)
    piece = shared_down.shape[0]
    gate_cols = by_core(shared_master[0].reshape(-1, FFS).astype(LOW), piece)
    up_cols = by_core(shared_master[1].reshape(-1, FFS).astype(LOW), piece)
    halves = [interleave(gate_cols[:, half], up_cols[:, half]) for half in range(2)]
    shared_rows = 2 * halves[0].shape[0]
    own_half = jnp.where(core == 0, halves[0], halves[1])
    far_half = to_sibling(jnp.where(core == 0, halves[1], halves[0]))
    near_gu = jnp.where(
        core == 0,
        jnp.concatenate([own_half, far_half], 0),
        jnp.concatenate([far_half, own_half], 0),
    )
    shared_packs = collect(gather_rows(pack(near_gu, shared_down), "ring"), "expert")
    whole_tiles = shared_rows % 16 == 0 and piece % 16 == 0

    router_low = router.astype(LOW)
    flat_ids = routes.reshape(-1)
    onehot = (flat_ids[:, None] == jnp.arange(experts_all, dtype=jnp.int32)[None, :]).astype(
        jnp.int32
    )
    slot_rank = jnp.sum((jnp.cumsum(onehot, 0) - onehot) * onehot, 1)
    target_row = jnp.where(
        slot_rank < capacity, flat_ids * capacity + slot_rank, experts_all * capacity
    ).reshape(tok_count, top_count)
    router_rows = jnp.zeros((128, model_width), LOW).at[:experts_all].set(router_low.T)

    cos, sin = rope_tables(tok_count)
    target_t = target_row.T
    query, key, value, heads, totals, normed, middle, branch_in = attend_forward(
        prefix, tokens_in, norm_gains, cos, sin, w_attn, [target_t, router_rows]
    )

    first_send, second_send, branch_t, cotangent_t = dispatch(
        here_ref, routes.T, target_t, branch_in, cotangent, router_rows[:16], owner_count,
        capacity,
    )
    first_rows = exchange(first_send, "expert")
    second_rows = exchange(second_send, "expert")
    turned_pair = [branch_in, cotangent, branch_t, cotangent_t]
    if whole_tiles:
        near_packs = wait_all(shared_packs, totals)
        far_packs = [to_sibling(stack) for stack in near_packs]
        shared_outs = swiglu_stacks(
            here_ref, *turned_pair, near_packs, far_packs, rings, shared_rows, piece, []
        )
    else:
        order = jnp.arange(owner_count) ^ here
        w_sgu, w_sd = unpack(
            jnp.take(jnp.stack(shared_packs), order, axis=0), shared_rows, piece
        )
        shared_outs = swiglu(
            *turned_pair, [w_sgu, to_sibling(w_sgu)], [w_sd, to_sibling(w_sd)]
        )
    shared_out, grad_branch_shared, grad_sgu, grad_sd, grad_sgu_far, grad_sd_far = shared_outs
    first_out, first_act, first_grad_act, first_turned = expert_pass(
        first_rows, expert_stack, [grad_branch_shared]
    )
    first_back = exchange(first_out, "expert")
    second_out, second_act, second_grad_act, second_turned = expert_pass(
        second_rows, expert_stack, [first_act]
    )
    second_back = exchange(second_out, "expert")
    far = [to_sibling(grad_sgu_far), to_sibling(grad_sd_far)]
    if whole_tiles:
        packs = pack_grads(
            here_ref, owner_count, [grad_sgu, grad_sd], far, rings, shared_rows, piece
        )
    else:
        pair_gu, pair_down = sum_low([grad_sgu, far[0]]), sum_low([grad_sd, far[1]])
        stacks = jnp.concatenate(
            [
                pack(
                    pair_gu[device * shared_rows : (device + 1) * shared_rows],
                    pair_down[device * piece : (device + 1) * piece],
                )
                for device in range(owner_count * rings)
            ],
            0,
        ).reshape(owner_count, -1, 256)
        stacks = jnp.take(stacks, order, axis=0)
        packs = [stacks[index] for index in range(owner_count)]
    turned = [first_turned, second_turned]
    grad_ed = weight_grad(turned, [first_act, second_act], 1, True, 512, first_back[1:])
    expert_down_low = scatter_rows(grad_ed, SHARD)
    grad_egu = weight_grad(
        turned, [first_grad_act, second_grad_act], 0, False, 1024, [grad_ed]
    )
    expert_gu_low = scatter_rows(grad_egu, SHARD)

    packs = wait_all(packs, grad_egu, *second_back[1:])
    (
        block_out, grad_middle, grad_attn_low, grad_attn_t, normed_t, grad_router_rows,
        grad_gain_rows,
    ) = combine(
        here_ref, routes, target_row, first_back, second_back, middle, shared_out,
        grad_branch_shared, cotangent, branch_in, normed, norm_gains, router_rows,
        [grad_egu, packs[0]],
    )

    grad_w, grad_normed = attend_backward(
        prefix, query, key, value, heads, totals, cos, sin, normed_t, grad_attn_low, grad_attn_t,
        w_attn,
    )
    quarters = exchange(packs, "expert")
    attn_sum = scatter_rows(
        wait_for(grad_w, expert_gu_low, expert_down_low, *quarters[1:]), SHARD
    )
    quarter = sum_low(quarters).reshape(rings, -1, 256)
    blocks = FFS // 256
    columns = quarter[:, : blocks * shared_rows].reshape(
        rings, blocks, 2, shared_rows // 2, 256
    )
    mine = jnp.where(core == 0, columns[:, :, 0], columns[:, :, 1])
    other = to_sibling(jnp.where(core == 0, columns[:, :, 1], columns[:, :, 0]))
    by_half = [jnp.where(core == half, mine, other) for half in range(2)]
    quarter = jnp.concatenate(
        [half.reshape(rings, -1, 256) for half in by_half]
        + [quarter[:, blocks * shared_rows :]],
        1,
    ).reshape(-1, 256)
    hidden_in = tokens_in.astype(WIDE)
    first_rms = rms_scale(hidden_in)
    first_hat = hidden_in * first_rms
    grad_first_gain = jnp.sum(grad_normed * first_hat, 0)
    tokens_grad = grad_middle + norm_back(grad_normed, first_hat, first_rms, norm_gains[0])

    small = jnp.concatenate(
        [
            grad_first_gain[None],
            jnp.sum(grad_gain_rows, 0, keepdims=True),
            grad_router_rows[:experts_all],
        ],
        0,
    )
    small_sum = add_up(small, EVERY)
    gain_grad = small_sum[:2]
    router_grad = small_sum[2:].T

    expert_new, expert_first_new, expert_second_new = (
        state[None]
        for state in expert_update(
            expert_gu_low,
            expert_down_low,
            [state[0] for state in (expert_master, expert_first, expert_second)],
        )
    )
    gains_new, gains_first_new, gains_second_new = adam_update(
        norm_gains, gains_first, gains_second, gain_grad, RATE_GAIN, 0.0
    )
    router_new, router_first_new, router_second_new = adam_update(
        router, router_first, router_second, router_grad, RATE_ROUTER, WEIGHT_DECAY
    )
    quarter, attn_sum = wait_all([quarter, attn_sum], gains_new, tokens_grad, expert_new)
    shared_low = scatter_rows(quarter, "ring")
    slot_grads = split_columns(attn_sum, slot_of, owner_count, own_count)
    owned_grad = sum(part.astype(WIDE) for part in exchange(slot_grads, "expert"))

    owned_count = jnp.sum((owners == lax.axis_index("expert")).astype(jnp.int32))
    slot_used = (jnp.arange(own_count, dtype=jnp.int32) < owned_count)[:, None, None]
    attn_w, attn_m, attn_n = adam_update(
        attn_master, attn_first, attn_second, owned_grad, RATE_ATTENTION, WEIGHT_DECAY
    )
    attn_new = jnp.where(slot_used, attn_w, 0.0)
    attn_first_new = jnp.where(slot_used, attn_m, 0.0)
    attn_second_new = jnp.where(slot_used, attn_n, 0.0)
    own_rows = shared_rows // 2
    shared_states = [shared_master, shared_first, shared_second]
    if whole_tiles and piece == 64 and own_rows % 8 == 0:
        shared_new, shared_first_new, shared_second_new = shared_update(
            shared_low, own_rows, piece, shared_states
        )
    else:
        top = 2 * blocks * own_rows
        by_half = (
            shared_low[:top]
            .reshape(2, blocks, own_rows, 256)
            .transpose(0, 2, 1, 3)
            .reshape(2, own_rows, FFS)
            .astype(WIDE)
        )
        parts = [deinterleave(by_half[half]) for half in range(2)]
        down = shared_low[top:].reshape(-1, piece, 256).transpose(1, 0, 2).astype(WIDE)
        shared_summed = jnp.stack(
            [
                from_core(jnp.stack([parts[0][kind], parts[1][kind]], 1), piece).reshape(-1, 128)
                for kind in range(2)
            ]
            + [down.reshape(-1, 128)]
        )
        shared_new, shared_first_new, shared_second_new = adam_update(
            *shared_states, shared_summed, RATE_MATRIX, WEIGHT_DECAY
        )
    copies = jnp.concatenate(collect(attn_new.astype(LOW), "expert"), 0)
    attn_copy = jnp.take(wait_for(copies, shared_new), slot_of, axis=0)
    return (
        block_out,
        tokens_grad,
        attn_new,
        attn_first_new,
        attn_second_new,
        attn_copy,
        expert_new,
        expert_first_new,
        expert_second_new,
        shared_new,
        shared_first_new,
        shared_second_new,
        gains_new,
        gains_first_new,
        gains_second_new,
        router_new,
        router_first_new,
        router_second_new,
    )


def solution(mesh):
    owner_count, shard_count = mesh.devices.shape
    fine = Mesh(mesh.devices.reshape(owner_count, shard_count // 2, 2), EVERY)
    tokens = P(EVERY, None)
    slots = P("expert", SHARD, None)
    experts = P("expert", None, SHARD, None)
    shared = P(None, EVERY, None)
    return jax.shard_map(
        body,
        mesh=fine,
        in_specs=(tokens,) * 3
        + (P(EVERY), P())
        + (slots,) * 3
        + (experts,) * 3
        + (shared,) * 3
        + (P(),) * 6,
        out_specs=(tokens,) * 2
        + (slots,) * 3
        + (P(None, SHARD, None),)
        + (experts,) * 3
        + (shared,) * 3
        + (P(),) * 6,
        check_vma=False,
    )
```

```python
import functools
import jax
import jax.numpy as jnp
from jax import lax
from jax.experimental import pallas as pl
from jax.experimental.pallas import tpu as pltpu
from jax.sharding import Mesh, PartitionSpec as P

HEADS = 12
HEAD_DIM = 64
FF = 2048
FFS = 2048
SEQ_LEN = 1024
STEP = 5

NORM_EPSILON = 1e-06
ADAM_EPSILON = 1e-08
FIRST_BETA = 0.5
SECOND_BETA = 0.5
WEIGHT_DECAY = 0.1
RATE_ATTENTION = 0.06
RATE_MATRIX = 0.03
RATE_ROUTER = 0.02
RATE_GAIN = 0.3
ROPE_BASE = 10000.0

PACK = 4
HALF = HEAD_DIM // 2
GROUP = PACK * HEAD_DIM
GROUPS = HEADS // PACK
BLOCK = 256
LONGEST_PREFIX = SEQ_LEN // 2
VMEM_BYTES = 60 * 1024 * 1024
AT_ONCE = pl.CostEstimate(flops=0, bytes_accessed=0, transcendentals=0)
LOW = jnp.bfloat16
WIDE = jnp.float32


def dot_nn(left, right):
    return jnp.dot(left, right, preferred_element_type=WIDE)


def dot_nt(left, right):
    return lax.dot_general(left, right, (((1,), (1,)), ((), ())), preferred_element_type=WIDE)


ANYWHERE = pl.BlockSpec(memory_space=pl.ANY)


def ignoring(kernel, first, count):
    return lambda *refs: kernel(*refs[:first], *refs[first + count :])


def side_by_side(ref):
    return jnp.concatenate([ref[piece] for piece in range(ref.shape[0])], 1)


def whole(shape):
    return pl.BlockSpec(shape, lambda *_: (0,) * len(shape))


def once(shape):
    return pl.BlockSpec(shape, lambda *_: (0,) * len(shape), pipeline_mode=pl.Buffered(1))


def params():
    return pltpu.CompilerParams(vmem_limit_bytes=VMEM_BYTES)


def chunk_of(shape):
    return (lax.broadcasted_iota(jnp.int32, shape, 1) & 127) >> 5


def gather_columns_kernel(slot_ref, slots_ref, out_ref, wide_ref):
    pairs = slots_ref.shape[1]
    chunk = chunk_of((pairs, 128))
    for group in range(GROUPS):
        for kind in range(4):
            parts = [
                slots_ref[slot_ref[kind * HEADS + group * PACK + head]].astype(WIDE)
                for head in range(PACK)
            ]
            for parity in range(2):
                for half in range(2):
                    source = 2 * parity + half
                    packed = None
                    for head in range(PACK):
                        shift = (head - source) * HALF % 128
                        moved = pltpu.roll(parts[head], shift, 1) if shift else parts[head]
                        packed = moved if head == 0 else jnp.where(chunk == head, moved, packed)
                    place = (group * 4 + kind) * 2 + half
                    wide_ref[place, pl.ds(parity, pairs, stride=2), :] = packed
    for place in range(wide_ref.shape[0]):
        out_ref[:, place * 128 : (place + 1) * 128] = wide_ref[place].astype(LOW)


def gather_columns(slots, slot_of):
    pairs = slots.shape[1]
    shape = (2 * pairs, GROUPS * 4 * GROUP)
    return pl.pallas_call(
        gather_columns_kernel,
        out_shape=jax.ShapeDtypeStruct(shape, LOW),
        in_specs=[pl.BlockSpec(memory_space=pltpu.SMEM), pl.BlockSpec(memory_space=pltpu.VMEM)],
        out_specs=pl.BlockSpec(memory_space=pltpu.VMEM),
        scratch_shapes=[pltpu.VMEM((shape[1] // 128, shape[0], 128), WIDE)],
        compiler_params=params(),
    )(slot_of, slots)


def split_columns_kernel(slot_ref, grad_ref, *refs):
    out_refs, slots_ref, wide_ref = refs[:-2], refs[-2], refs[-1]
    slots, pairs, _ = slots_ref.shape
    chunk = chunk_of((pairs, 128))
    slots_ref[...] = jnp.zeros_like(slots_ref)
    for group in range(GROUPS):
        first = group * 4 * GROUP
        for place in range(wide_ref.shape[0]):
            columns = slice(first + place * 128, first + (place + 1) * 128)
            wide_ref[place] = grad_ref[:, columns].astype(WIDE)
        for kind in range(4):
            blocks = [
                wide_ref[kind * 2 + source % 2, pl.ds(source // 2, pairs, stride=2), :]
                for source in range(4)
            ]
            for head in range(PACK):
                packed = None
                for source in range(4):
                    shift = (source - head) * HALF % 128
                    moved = pltpu.roll(blocks[source], shift, 1) if shift else blocks[source]
                    packed = moved if source == 0 else jnp.where(chunk == source, moved, packed)
                slots_ref[slot_ref[kind * HEADS + group * PACK + head]] = packed.astype(LOW)
    held = slots // len(out_refs)
    for index, out_ref in enumerate(out_refs):
        out_ref[...] = slots_ref[index * held : (index + 1) * held]


def split_columns(grad, slot_of, partners, held):
    rows = grad.shape[0]
    shape = (held, rows // 2, 128)
    return pl.pallas_call(
        split_columns_kernel,
        out_shape=[jax.ShapeDtypeStruct(shape, LOW)] * partners,
        in_specs=[pl.BlockSpec(memory_space=pltpu.SMEM), pl.BlockSpec(memory_space=pltpu.VMEM)],
        out_specs=[pl.BlockSpec(memory_space=pltpu.VMEM)] * partners,
        scratch_shapes=[
            pltpu.VMEM((partners * held, rows // 2, 128), LOW),
            pltpu.VMEM((4 * GROUP // 128, rows, 128), WIDE),
        ],
        compiler_params=params(),
    )(slot_of, grad)


def key_extent(block):
    return max((block + 1) * BLOCK, LONGEST_PREFIX)


def attend_forward_kernel(
    prefix_ref, token_ref, gain_ref, cos_ref, sin_ref, w_ref,
    query_ref, key_ref, value_ref, head_ref, rest_ref, total_ref, normed_ref, middle_ref,
    branch_ref, sum_ref,
):
    group = pl.program_id(0)
    length, width = token_ref.shape

    @pl.when(group == 0)
    def _():
        hidden = token_ref[...].astype(WIDE)
        scale = lax.rsqrt(jnp.mean(hidden * hidden, -1, keepdims=True) + NORM_EPSILON)
        normed_ref[...] = (hidden * scale * gain_ref[0:1, :]).astype(LOW)
        middle_ref[...] = hidden
        total_ref[...] = jnp.zeros_like(total_ref)

    projected = dot_nn(normed_ref[...], w_ref[:, : 3 * GROUP])
    cos, sin = cos_ref[...], sin_ref[...]
    for kind, ref in enumerate((query_ref, key_ref)):
        lead = projected[:, kind * GROUP : kind * GROUP + 128]
        tail = projected[:, kind * GROUP + 128 : (kind + 1) * GROUP]
        ref[:, :128] = (lead * cos - tail * sin).astype(LOW)
        ref[:, 128:] = (tail * cos + lead * sin).astype(LOW)
    value_ref[...] = projected[:, 2 * GROUP :].astype(LOW)
    prefix = prefix_ref[0]

    lane = lax.broadcasted_iota(jnp.int32, (1, GROUP), 1)
    total_lane = lax.broadcasted_iota(jnp.int32, (BLOCK, 128), 1)
    owned = [chunk_of((1, GROUP)) == head for head in range(PACK)]
    ones = [lane == (head + 1) % PACK * HALF for head in range(PACK)]
    items = [(head, block) for head in range(PACK) for block in range(length // BLOCK)]

    def score(head, block):
        rows = slice(block * BLOCK, (block + 1) * BLOCK)
        own = owned[head].astype(WIDE).astype(LOW)
        return dot_nt(
            query_ref[rows, :] * (own * HEAD_DIM ** (-0.5)), key_ref[: key_extent(block), :]
        )

    def attend(head, block, scores):
        start = block * BLOCK
        rows = slice(start, start + BLOCK)
        edge = scores[:, start:]
        key_pos = lax.broadcasted_iota(jnp.int32, edge.shape, 1)
        allowed = key_pos <= lax.broadcasted_iota(jnp.int32, edge.shape, 0)
        if start < LONGEST_PREFIX:
            allowed = allowed | (key_pos < prefix - start)
        edge = jnp.where(allowed, edge, -1e30)
        scores = jnp.concatenate([scores[:, :start], edge], 1) if start else edge
        peak = jnp.max(scores, -1, keepdims=True)
        weights = jnp.exp(scores - peak).astype(LOW)
        own = owned[head].astype(WIDE).astype(LOW)
        values = value_ref[: key_extent(block), :] * own + ones[head].astype(WIDE).astype(LOW)
        mixed = dot_nn(weights, values)
        total = jnp.sum(jnp.where(ones[head], mixed, 0.0), -1, keepdims=True)
        mixed = jnp.where(owned[head], mixed * (1.0 / total), 0.0)
        sum_ref[rows, :] = mixed if head == 0 else sum_ref[rows, :] + mixed
        total_ref[rows, :] = jnp.where(
            total_lane == group * PACK + head, peak + jnp.log(total), total_ref[rows, :]
        )

    ahead = score(*items[0])
    for index, item in enumerate(items):
        scores = ahead
        if index + 1 < len(items):
            ahead = score(*items[index + 1])
        attend(*item, scores)
    heads = sum_ref[...].astype(LOW)
    head_ref[...] = heads
    rest_ref[...] = (sum_ref[...] - heads.astype(WIDE)).astype(LOW)
    middle_ref[...] += dot_nt(heads, w_ref[:, 3 * GROUP :])

    @pl.when(group == pl.num_programs(0) - 1)
    def _():
        middle = middle_ref[...]
        scale = lax.rsqrt(jnp.mean(middle * middle, -1, keepdims=True) + NORM_EPSILON)
        branch_ref[...] = (middle * scale * gain_ref[1:2, :]).astype(LOW)


def attend_forward(prefix, tokens, gains, cos, sin, w_attn, after):
    length, width = tokens.shape
    low = lambda columns: jax.ShapeDtypeStruct((length, columns), LOW)
    grouped = pl.BlockSpec((length, GROUP), lambda group: (0, group))
    return pl.pallas_call(
        ignoring(attend_forward_kernel, 6, len(after)),
        grid=(GROUPS,),
        out_shape=[
            low(width), low(width), low(width), low(width), low(width),
            jax.ShapeDtypeStruct((length, 128), WIDE),
            low(width),
            jax.ShapeDtypeStruct((length, width), WIDE),
            low(width),
        ],
        in_specs=[
            pl.BlockSpec(memory_space=pltpu.SMEM),
            once(tokens.shape),
            once(gains.shape),
            once(cos.shape),
            once(sin.shape),
            pl.BlockSpec((width, 4 * GROUP), lambda group: (0, group)),
        ]
        + [ANYWHERE] * len(after),
        out_specs=[
            grouped, grouped, grouped, grouped, grouped,
            whole((length, 128)),
            whole((length, width)),
            whole((length, width)),
            whole((length, width)),
        ],
        scratch_shapes=[pltpu.VMEM((length, GROUP), WIDE)],
        compiler_params=params(),
        cost_estimate=pl.CostEstimate(
            flops=25_000_000_000, bytes_accessed=20_000_000, transcendentals=9_000_000
        ),
    )(prefix, tokens, gains, cos, sin, w_attn, *after)


def attend_backward_kernel(
    prefix_ref, query_ref, key_ref, value_ref, head_ref, rest_ref, total_ref, cos_ref, sin_ref,
    normed_t_ref, grad_ref, grad_t_ref, w_ref, grad_w_ref, grad_normed_ref,
    total_t_ref, scaled_ref, key_t_ref, grad_head_ref, center_ref,
    probs_ref, grad_scores_ref, grad_query_t_ref, grad_key_ref, grad_value_ref,
):
    step = pl.program_id(0)
    length = query_ref.shape[0]

    @pl.when(step == 0)
    def _():
        total_t_ref[...] = total_ref[...].T
        grad_normed_ref[...] = jnp.zeros_like(grad_normed_ref)

    scaled_ref[...] = query_ref[...] * HEAD_DIM ** (-0.5)
    key_t = key_ref[...].T
    for head in range(PACK):
        for half in range(2):
            first = half * 128 + head * HALF
            key_t_ref[head, half * HALF : (half + 1) * HALF, :] = key_t[first : first + HALF]
    grad_heads = dot_nn(grad_ref[...], w_ref[:, 3 * GROUP :]).astype(LOW)
    grad_head_ref[...] = grad_heads
    product = grad_heads.astype(WIDE) * (head_ref[...].astype(WIDE) + rest_ref[...].astype(WIDE))
    leading = product.astype(LOW)
    rest = (product - leading.astype(WIDE)).astype(LOW)
    head_row = lax.broadcasted_iota(jnp.int32, (16, GROUP), 0)
    select = (chunk_of((16, GROUP)) == head_row).astype(WIDE).astype(LOW)
    center_ref[...] = dot_nt(select, leading) + dot_nt(select, rest)
    prefix = prefix_ref[0]
    owned = [(chunk_of((1, GROUP)) == head).astype(WIDE).astype(LOW) for head in range(PACK)]
    items = [(head, block) for head in range(PACK) for block in range(length // BLOCK)]

    def score(head, block):
        rows = slice(block * BLOCK, (block + 1) * BLOCK)
        extent = key_extent(block)
        return (
            dot_nt(key_ref[:extent, :], scaled_ref[rows, :] * owned[head]),
            dot_nt(value_ref[:extent, :], grad_head_ref[rows, :] * owned[head]),
        )

    def weigh(head, block, scores, grad_probs):
        start, extent = block * BLOCK, key_extent(block)
        rows = slice(start, start + BLOCK)
        totals = total_t_ref[pl.ds(step * PACK + head, 1), rows]
        probs = jnp.exp(scores - totals)
        edge = probs[start:, :]
        key_pos = lax.broadcasted_iota(jnp.int32, edge.shape, 0)
        allowed = key_pos <= lax.broadcasted_iota(jnp.int32, edge.shape, 1)
        if start < LONGEST_PREFIX:
            allowed = allowed | (key_pos < prefix - start)
        edge = jnp.where(allowed, edge, 0.0)
        probs = jnp.concatenate([probs[:start, :], edge], 0) if start else edge
        grad_scores = (probs * (grad_probs - center_ref[head : head + 1, rows])).astype(LOW)
        probs_ref[head % 2, :extent, rows] = probs.astype(LOW)
        grad_scores_ref[head % 2, :extent, rows] = grad_scores
        grad_query_t = dot_nn(key_t_ref[head, :, :extent], grad_scores)
        for half in range(2):
            first = half * 128 + head * HALF
            grad_query_t_ref[first : first + HALF, rows] = grad_query_t[
                half * HALF : (half + 1) * HALF
            ]

    def gather_keys(head):
        queries, grads = scaled_ref[...] * owned[head], grad_head_ref[...] * owned[head]
        first = 0
        while first < length:
            seen = 0 if first < LONGEST_PREFIX else first
            keys = slice(first, LONGEST_PREFIX if first < LONGEST_PREFIX else first + BLOCK)
            for ref, source, right in (
                (grad_value_ref, probs_ref, grads),
                (grad_key_ref, grad_scores_ref, queries),
            ):
                part = dot_nn(source[head % 2, keys, seen:], right[seen:, :])
                ref[keys, :] = part if head == 0 else ref[keys, :] + part
            first = keys.stop

    ahead = score(*items[0])
    for index, (head, block) in enumerate(items):
        scores = ahead
        if index + 1 < len(items):
            ahead = score(*items[index + 1])
        weigh(head, block, *scores)
        if (block + 1) * BLOCK == length:
            gather_keys(head)
    cos, sin = cos_ref[...], sin_ref[...]
    pieces = []
    for grad in (grad_query_t_ref[...].T * HEAD_DIM ** (-0.5), grad_key_ref[...]):
        lead, tail = grad[:, :128], grad[:, 128:]
        pieces.append((lead * cos + tail * sin).astype(LOW))
        pieces.append((tail * cos - lead * sin).astype(LOW))
    pieces.append(grad_value_ref[...].astype(LOW))
    grads = jnp.concatenate(pieces, 1)
    grad_w_ref[:, : 3 * GROUP] = dot_nn(side_by_side(normed_t_ref), grads).astype(LOW)
    grad_w_ref[:, 3 * GROUP :] = dot_nn(side_by_side(grad_t_ref), head_ref[...]).astype(LOW)
    grad_normed_ref[...] += dot_nt(grads, w_ref[:, : 3 * GROUP])


def attend_backward(
    prefix, query, key, value, heads, rest, totals, cos, sin, normed_t, grad, grad_t, w_attn
):
    length, width = grad.shape
    grouped = pl.BlockSpec((length, GROUP), lambda step: (0, step))
    return pl.pallas_call(
        attend_backward_kernel,
        grid=(GROUPS,),
        out_shape=[
            jax.ShapeDtypeStruct((width, GROUPS * 4 * GROUP), LOW),
            jax.ShapeDtypeStruct((length, width), WIDE),
        ],
        in_specs=[
            pl.BlockSpec(memory_space=pltpu.SMEM),
            grouped, grouped, grouped, grouped, grouped,
            once(totals.shape), once(cos.shape), once(sin.shape), once(normed_t.shape),
            once(grad.shape), once(grad_t.shape),
            pl.BlockSpec((width, 4 * GROUP), lambda step: (0, step)),
        ],
        out_specs=[
            pl.BlockSpec((width, 4 * GROUP), lambda step: (0, step)),
            whole((length, width)),
        ],
        scratch_shapes=[
            pltpu.VMEM((128, length), WIDE),
            pltpu.VMEM((length, GROUP), LOW),
            pltpu.VMEM((PACK, HEAD_DIM, length), LOW),
            pltpu.VMEM((length, GROUP), LOW),
            pltpu.VMEM((16, length), WIDE),
            pltpu.VMEM((2, length, length), LOW),
            pltpu.VMEM((2, length, length), LOW),
            pltpu.VMEM((GROUP, length), WIDE),
            pltpu.VMEM((length, GROUP), WIDE),
            pltpu.VMEM((length, GROUP), WIDE),
        ],
        compiler_params=params(),
        cost_estimate=AT_ONCE,
    )(prefix, query, key, value, heads, rest, totals, cos, sin, normed_t, grad, grad_t, w_attn)


def swiglu_blocks(blocks, rows_of, w_gu_ref, w_d_ref, act_ref, grad_act_ref, sum_ref, grad_sum_ref):
    subs = w_d_ref.shape[0] // HIDDEN_BLOCK
    items = [(block, sub) for block in range(blocks) for sub in range(subs)]

    def into(block, sub):
        _, tokens, grads_in = rows_of(block)
        units = slice(sub * HIDDEN_BLOCK, (sub + 1) * HIDDEN_BLOCK)
        both = slice(2 * sub * HIDDEN_BLOCK, 2 * (sub + 1) * HIDDEN_BLOCK)
        return dot_nn(tokens, w_gu_ref[:, both]), dot_nt(grads_in, w_d_ref[units, :])

    def middle(block, sub, gate_up, grad_hidden):
        rows, _, _ = rows_of(block)
        units = slice(sub * HIDDEN_BLOCK, (sub + 1) * HIDDEN_BLOCK)
        both = slice(2 * sub * HIDDEN_BLOCK, 2 * (sub + 1) * HIDDEN_BLOCK)
        gate, up = gate_up[:, :HIDDEN_BLOCK], gate_up[:, HIDDEN_BLOCK:]
        sig = 0.5 * jnp.tanh(0.5 * gate) + 0.5
        act = gate * sig
        act_ref[rows, units] = (act * up).astype(LOW)
        grad_act_ref[rows, both] = jnp.concatenate(
            [
                (grad_hidden * up * (sig + act * (1.0 - sig))).astype(LOW),
                (grad_hidden * act).astype(LOW),
            ],
            1,
        )

    def out(block):
        rows, _, _ = rows_of(block)
        sum_ref[rows, :] += dot_nn(act_ref[rows, :], w_d_ref[...])
        grad_sum_ref[rows, :] += dot_nt(grad_act_ref[rows, :], w_gu_ref[...])

    ahead = into(*items[0])
    for index, item in enumerate(items):
        products = ahead
        if index + 1 < len(items):
            ahead = into(*items[index + 1])
        middle(*item, *products)
        if item[1] == subs - 1:
            out(item[0])


def swiglu_kernel(parts, rows_ref, grad_ref, rows_t_ref, grad_t_ref, *refs):
    w_gu_refs, w_d_refs, refs = refs[:parts], refs[parts : 2 * parts], refs[2 * parts :]
    out_ref, grad_rows_ref, refs = refs[0], refs[1], refs[2:]
    grad_gu_refs, grad_d_refs = refs[0 : 2 * parts : 2], refs[1 : 2 * parts : 2]
    act_ref, grad_act_ref = refs[2 * parts :]
    step = pl.program_id(0)
    count = rows_ref.shape[0]
    per_part = pl.num_programs(0) // parts

    @pl.when(step == 0)
    def _():
        out_ref[...] = jnp.zeros_like(out_ref)
        grad_rows_ref[...] = jnp.zeros_like(grad_rows_ref)

    def one_part(w_gu_ref, w_d_ref, grad_gu_ref, grad_d_ref):
        def rows_of(block):
            rows = slice(block * ROW_BLOCK, (block + 1) * ROW_BLOCK)
            return rows, rows_ref[rows, :], grad_ref[rows, :]

        swiglu_blocks(
            count // ROW_BLOCK, rows_of, w_gu_ref, w_d_ref, act_ref, grad_act_ref, out_ref,
            grad_rows_ref,
        )
        grad_gu_ref[...] = dot_nn(side_by_side(rows_t_ref), grad_act_ref[...]).astype(LOW)
        grad_d_ref[...] = dot_nn(side_by_side(grad_t_ref), act_ref[...]).astype(LOW).T

    for part in range(parts):
        pl.when(step // per_part == part)(
            functools.partial(
                one_part, w_gu_refs[part], w_d_refs[part], grad_gu_refs[part], grad_d_refs[part]
            )
        )


ROW_BLOCK = 512
HIDDEN_BLOCK = 256


def swiglu(rows, grad, rows_t, grad_t, w_gu, w_d):
    count, width = rows.shape
    parts = len(w_d)
    hidden = w_d[0].shape[0]
    chunk = EXPERT_BLOCK
    per_part = hidden // chunk

    def place(part):
        return lambda step: jnp.clip(step - part * per_part, 0, per_part - 1)

    gu_specs = [
        pl.BlockSpec((width, 2 * chunk), lambda step, at=place(part): (0, at(step)))
        for part in range(parts)
    ]
    d_specs = [
        pl.BlockSpec((chunk, width), lambda step, at=place(part): (at(step), 0))
        for part in range(parts)
    ]
    gu_shape = jax.ShapeDtypeStruct((width, 2 * hidden), LOW)
    d_shape = jax.ShapeDtypeStruct((hidden, width), LOW)
    total = parts * hidden
    return pl.pallas_call(
        functools.partial(swiglu_kernel, parts),
        grid=(parts * per_part,),
        out_shape=[jax.ShapeDtypeStruct((count, width), WIDE)] * 2 + [gu_shape, d_shape] * parts,
        in_specs=[once(each.shape) for each in (rows, grad, rows_t, grad_t)] + gu_specs + d_specs,
        out_specs=[whole((count, width))] * 2
        + [spec for pair in zip(gu_specs, d_specs) for spec in pair],
        scratch_shapes=[
            pltpu.VMEM((count, chunk), LOW),
            pltpu.VMEM((count, 2 * chunk), LOW),
        ],
        compiler_params=params(),
        cost_estimate=pl.CostEstimate(
            flops=18 * count * width * total,
            bytes_accessed=12 * width * total + 12 * count * width,
            transcendentals=count * total,
        ),
    )(rows, grad, rows_t, grad_t, *w_gu, *w_d)


def wait_all(values, *others):
    count = len(values)
    anywhere = pl.BlockSpec(memory_space=pl.ANY)
    return pl.pallas_call(
        lambda *refs: None,
        out_shape=[jax.ShapeDtypeStruct(value.shape, value.dtype) for value in values],
        in_specs=[anywhere] * (count + len(others)),
        out_specs=[anywhere] * count,
        input_output_aliases={index: index for index in range(count)},
        cost_estimate=AT_ONCE,
    )(*values, *others)


def wait_for(value, *others):
    return wait_all([value], *others)[0]


def pair_gates(chosen):
    peak = functools.reduce(jnp.maximum, chosen)
    weights = [jnp.exp(each - peak) for each in chosen]
    total = sum(weights[1:], weights[0])
    return [each / total for each in weights]


def dispatch_kernel(
    here_ref, route_ref, target_ref, branch_ref, grad_ref, router_ref, *refs
):
    partner = pl.program_id(0)
    partners = (len(refs) - 3) // 2
    turned_refs, gate_ref = refs[-3:-1], refs[-1]
    top, count = route_ref.shape
    half = refs[0].shape[1]
    capacity = 2 * half

    @pl.when(partner == 0)
    def _():
        logits = dot_nt(router_ref[...], branch_ref[...])
        row = lax.broadcasted_iota(jnp.int32, logits.shape, 0)
        chosen = [
            jnp.sum(jnp.where(row == route_ref[pick : pick + 1, :], logits, 0.0), 0, keepdims=True)
            for pick in range(top)
        ]
        for pick, gate in enumerate(pair_gates(chosen)):
            gate_ref[pick : pick + 1, :] = gate

    piece = pl.ds(pl.multiple_of(jnp.minimum(partner, count // BLOCK - 1) * BLOCK, BLOCK), BLOCK)
    for source_ref, turned_ref in zip((branch_ref, grad_ref), turned_refs):
        turned_ref[0] = source_ref[piece, :].T
    expert = here_ref[0] ^ partner
    place = expert * capacity + lax.broadcasted_iota(jnp.int32, (capacity, count), 0)
    spread = jnp.zeros((capacity, count), WIDE)
    gates = jnp.zeros((capacity, count), WIDE)
    for pick in range(top):
        here = target_ref[pick : pick + 1, :] == place
        spread = jnp.where(here, 1.0, spread)
        gates = jnp.where(here, gate_ref[pick : pick + 1, :], gates)
    spread = spread.astype(LOW)
    rows = dot_nn(spread, branch_ref[...]).astype(LOW)
    grads = dot_nn(spread, grad_ref[...])
    grads = (grads * jnp.sum(gates, 1, keepdims=True)).astype(LOW)

    def store(first_ref, second_ref):
        for ref, part in ((first_ref, slice(0, half)), (second_ref, slice(half, capacity))):
            ref[0] = rows[part]
            ref[1] = grads[part]

    for index in range(partners):
        pl.when(partner == index)(
            functools.partial(store, refs[index], refs[partners + index])
        )


def dispatch(here, routes_t, target_t, branch_in, grad, router_t, partners, capacity):
    count, width = branch_in.shape
    top = routes_t.shape[0]
    shape = (2, capacity // 2, width)
    outs = pl.pallas_call(
        dispatch_kernel,
        grid=(partners,),
        out_shape=[jax.ShapeDtypeStruct(shape, LOW)] * (2 * partners)
        + [jax.ShapeDtypeStruct((count // BLOCK, width, BLOCK), LOW)] * 2
        + [jax.ShapeDtypeStruct((top, count), WIDE)],
        in_specs=[
            pl.BlockSpec(memory_space=pltpu.SMEM),
            once(routes_t.shape), once(target_t.shape), once(branch_in.shape), once(grad.shape),
            once(router_t.shape),
        ],
        out_specs=[whole(shape)] * (2 * partners)
        + [
            pl.BlockSpec(
                (1, width, BLOCK), lambda step: (jnp.minimum(step, count // BLOCK - 1), 0, 0)
            )
        ]
        * 2
        + [whole((top, count))],
        compiler_params=params(),
        cost_estimate=pl.CostEstimate(
            flops=4 * partners * capacity * count * width,
            bytes_accessed=4 * (partners * capacity + count) * width,
            transcendentals=0,
        ),
    )(here, routes_t, target_t, branch_in, grad, router_t)
    return outs[:partners], outs[partners : 2 * partners], *outs[2 * partners : -1]


def expert_kernel(sources, *refs):
    rows_refs, refs = refs[:sources], refs[sources:]
    gu_stack_ref, d_stack_ref, refs = refs[0], refs[1], refs[2:]
    out_refs, refs = refs[:sources], refs[sources:]
    act_ref, grad_act_ref, turned_ref, out_sum_ref, grad_sum_ref, w_gu_ref, w_d_ref = refs
    step = pl.program_id(0)
    _, per_source, width = rows_refs[0].shape
    block = max(1, ROW_BLOCK // per_source)
    count = block * per_source

    @pl.when(step == 0)
    def _():
        out_sum_ref[...] = jnp.zeros_like(out_sum_ref)
        grad_sum_ref[...] = jnp.zeros_like(grad_sum_ref)

    for stack_ref, w_ref in ((gu_stack_ref, w_gu_ref), (d_stack_ref, w_d_ref)):
        columns = w_ref.shape[1] // 256
        tall = stack_ref.shape[1] // columns
        for column in range(columns):
            w_ref[:, column * 256 : (column + 1) * 256] = stack_ref[
                :, column * tall : (column + 1) * tall, :
            ].reshape(w_ref.shape[0], 256)

    def gather(index, member):
        return jnp.concatenate(
            [ref[member] for ref in rows_refs[index * block : (index + 1) * block]], 0
        )

    def rows_of(index):
        return slice(index * count, (index + 1) * count), gather(index, 0), gather(index, 1)

    swiglu_blocks(
        sources // block, rows_of, w_gu_ref, w_d_ref, act_ref, grad_act_ref, out_sum_ref,
        grad_sum_ref,
    )
    for piece in range(2 * (sources // block)):

        @pl.when(step == piece)
        def _():
            turned_ref[0, 0] = gather(piece % (sources // block), piece // (sources // block)).T

    @pl.when(step == pl.num_programs(0) - 1)
    def _():
        for index, ref in enumerate(out_refs):
            rows = slice(index * per_source, (index + 1) * per_source)
            ref[0] = out_sum_ref[rows, :].astype(LOW)
            ref[1] = grad_sum_ref[rows, :].astype(LOW)


EXPERT_BLOCK = 512


def expert_pass(rows, stack, after):
    sources = len(rows)
    _, per_source, width = rows[0].shape
    count = sources * per_source
    devices = stack.shape[0]
    chunk = EXPERT_BLOCK
    hidden = FF
    steps = hidden // chunk
    gu_tall = 2 * chunk // 256 * (width // devices)
    d_tall = width // 256 * (hidden // devices)
    blocks = 2 * count // ROW_BLOCK
    assert steps >= blocks and gu_tall * steps % d_tall == 0
    outs = pl.pallas_call(
        ignoring(functools.partial(expert_kernel, sources), sources + 2, len(after)),
        grid=(steps,),
        out_shape=[jax.ShapeDtypeStruct(rows[0].shape, LOW)] * sources
        + [
            jax.ShapeDtypeStruct((count, hidden), LOW),
            jax.ShapeDtypeStruct((count, 2 * hidden), LOW),
            jax.ShapeDtypeStruct((2, blocks // 2, width, ROW_BLOCK), LOW),
        ],
        in_specs=[once(rows[0].shape)] * sources
        + [
            pl.BlockSpec((devices, gu_tall, 256), lambda step: (0, step, 0)),
            pl.BlockSpec(
                (chunk * devices // hidden, d_tall, 256),
                lambda step: (step, gu_tall * steps // d_tall, 0),
            ),
        ]
        + [ANYWHERE] * len(after),
        out_specs=[whole(rows[0].shape)] * sources
        + [
            pl.BlockSpec((count, chunk), lambda step: (0, step)),
            pl.BlockSpec((count, 2 * chunk), lambda step: (0, step)),
            pl.BlockSpec(
                (1, 1, width, ROW_BLOCK),
                lambda step: (
                    jnp.minimum(step, blocks - 1) // (blocks // 2),
                    jnp.minimum(step, blocks - 1) % (blocks // 2),
                    0,
                    0,
                ),
            ),
        ],
        scratch_shapes=[
            pltpu.VMEM((count, width), WIDE),
            pltpu.VMEM((count, width), WIDE),
            pltpu.VMEM((width, 2 * chunk), LOW),
            pltpu.VMEM((chunk, width), LOW),
        ],
        compiler_params=params(),
        cost_estimate=pl.CostEstimate(
            flops=count * width * hidden, bytes_accessed=width * hidden, transcendentals=0
        ),
    )(*rows, stack, stack, *after)
    return outs[:sources], *outs[sources:]


def weight_grad_kernel(halves, turned, *refs):
    row_refs, act_refs, out_ref = refs[:halves], refs[halves : 2 * halves], refs[-1]
    rows_t = jnp.concatenate([side_by_side(ref.at[0]) for ref in row_refs], 1)
    grad = dot_nn(rows_t, jnp.concatenate([ref[...] for ref in act_refs], 0)).astype(LOW)
    out_ref[...] = grad.T if turned else grad


def weight_grad(rows, acts, member, turned, chunk, after):
    halves = len(acts)
    _, blocks, width, _ = rows[0].shape
    count, units = acts[0].shape
    member_spec = pl.BlockSpec(
        (1, blocks, width, ROW_BLOCK),
        lambda step: (member, 0, 0, 0),
        pipeline_mode=pl.Buffered(1),
    )
    return pl.pallas_call(
        ignoring(
            functools.partial(weight_grad_kernel, halves, turned), 2 * halves, len(after)
        ),
        grid=(units // chunk,),
        out_shape=jax.ShapeDtypeStruct((units, width) if turned else (width, units), LOW),
        in_specs=[member_spec] * halves
        + [pl.BlockSpec((count, chunk), lambda step: (0, step))] * halves
        + [ANYWHERE] * len(after),
        out_specs=pl.BlockSpec((chunk, width), lambda step: (step, 0))
        if turned
        else pl.BlockSpec((width, chunk), lambda step: (0, step)),
        compiler_params=params(),
        cost_estimate=pl.CostEstimate(
            flops=count * width * units // 8, bytes_accessed=width * units // 2, transcendentals=0
        ),
    )(*rows, *acts, *after)


def combine_kernel(
    partners, here_ref, route_ref, target_ref, middle_ref, shared_ref, grad_shared_ref,
    cotangent_ref, branch_ref, normed_ref, gain_ref, router_ref, *refs
):
    halves, refs = (refs[:partners], refs[partners : 2 * partners]), refs[2 * partners :]
    out_ref, grad_ref, grad_low_ref, grad_t_ref, normed_t_ref, grad_router_ref, grad_gain_ref = refs
    normed_t_ref[0] = normed_ref[...].T
    block, top = target_ref.shape
    _, half, width = halves[0][0].shape

    @pl.when(pl.program_id(0) == 0)
    def _():
        grad_router_ref[...] = jnp.zeros_like(grad_router_ref)
        grad_gain_ref[...] = jnp.zeros_like(grad_gain_ref)

    branch = branch_ref[...]
    logits = dot_nt(branch, router_ref[...])
    lane = lax.broadcasted_iota(jnp.int32, logits.shape, 1)
    picked_lane = [lane == route_ref[:, pick : pick + 1] for pick in range(top)]
    gates = pair_gates(
        [jnp.sum(jnp.where(here, logits, 0.0), 1, keepdims=True) for here in picked_lane]
    )
    slot = lax.broadcasted_iota(jnp.int32, (1, partners * half), 1)
    slot = ((slot // half) ^ here_ref[0]) * (2 * half) + slot % half
    picked, grad_rows = 0.0, 0.0
    for index, part in enumerate(halves):
        spread = [
            (target_ref[:, pick : pick + 1] == slot + index * half).astype(WIDE)
            for pick in range(top)
        ]
        stacked = jnp.concatenate(spread, 0).astype(LOW)
        outs, grads = (jnp.concatenate([ref[member] for ref in part], 0) for member in range(2))
        picked = picked + dot_nn(stacked, outs)
        grad_rows = grad_rows + dot_nn(sum(spread[1:], spread[0]).astype(LOW), grads)
    picked = [picked[pick * block : (pick + 1) * block] for pick in range(top)]
    middle = middle_ref[...]
    mixed = sum(gate * rows for gate, rows in zip(gates, picked))
    out_ref[...] = (middle + shared_ref[...] + mixed).astype(LOW)
    cotangent = cotangent_ref[...].astype(WIDE)
    grad_gates = [jnp.sum(cotangent * rows, 1, keepdims=True) for rows in picked]
    mean = sum(gate * grad for gate, grad in zip(gates, grad_gates))
    grad_logits = sum(
        jnp.where(here, gate * (grad - mean), 0.0)
        for here, gate, grad in zip(picked_lane, gates, grad_gates)
    ).astype(LOW)
    grad_router_ref[...] += lax.dot_general(
        grad_logits, branch, (((0,), (0,)), ((), ())), preferred_element_type=WIDE
    )
    grad_branch = grad_shared_ref[...] + dot_nn(grad_logits, router_ref[...]) + grad_rows
    scale = lax.rsqrt(jnp.mean(middle * middle, -1, keepdims=True) + NORM_EPSILON)
    hat = middle * scale
    grad_gain_ref[...] += jnp.sum((grad_branch * hat).reshape(block // 8, 8, width), 0)
    grad_hat = grad_branch * gain_ref[1:2, :]
    grad = cotangent + scale * (grad_hat - hat * jnp.mean(grad_hat * hat, -1, keepdims=True))
    grad_ref[...] = grad
    grad_low_ref[...] = grad.astype(LOW)
    grad_t_ref[0] = grad.astype(LOW).T


def combine(
    here, routes, target, first, second, middle, shared_out, grad_shared, cotangent, branch_in,
    normed, gains, router_t, after
):
    count, width = middle.shape
    top = routes.shape[1]
    lanes = router_t.shape[0]
    partners = len(first)
    rows = pl.BlockSpec((BLOCK, width), lambda step: (step, 0))
    pairs = pl.BlockSpec((BLOCK, top), lambda step: (step, 0))
    return pl.pallas_call(
        ignoring(
            functools.partial(combine_kernel, partners), 11 + 2 * partners, len(after)
        ),
        grid=(count // BLOCK,),
        out_shape=[
            jax.ShapeDtypeStruct((count, width), LOW),
            jax.ShapeDtypeStruct((count, width), WIDE),
            jax.ShapeDtypeStruct((count, width), LOW),
            jax.ShapeDtypeStruct((count // BLOCK, width, BLOCK), LOW),
            jax.ShapeDtypeStruct((count // BLOCK, width, BLOCK), LOW),
            jax.ShapeDtypeStruct((lanes, width), WIDE),
            jax.ShapeDtypeStruct((8, width), WIDE),
        ],
        in_specs=[
            pl.BlockSpec(memory_space=pltpu.SMEM),
            pairs, pairs, rows, rows, rows, rows, rows, rows,
            once(gains.shape), once(router_t.shape),
        ]
        + [once(first[0].shape)] * (2 * partners)
        + [ANYWHERE] * len(after),
        out_specs=[
            rows, rows, rows,
            pl.BlockSpec((1, width, BLOCK), lambda step: (step, 0, 0)),
            pl.BlockSpec((1, width, BLOCK), lambda step: (step, 0, 0)),
            whole((lanes, width)), whole((8, width)),
        ],
        compiler_params=params(),
        cost_estimate=pl.CostEstimate(
            flops=400_000_000_000, bytes_accessed=25_000_000, transcendentals=0
        ),
    )(
        here, routes, target, middle, shared_out, grad_shared, cotangent, branch_in, normed,
        gains, router_t, *first, *second, *after
    )


def swiglu_stacks_kernel(
    partners, rings, col_rows, piece, here_ref, rows_ref, grad_ref, rows_t_ref, grad_t_ref, *refs
):
    stacks, refs = refs[: 4 * partners], refs[4 * partners :]
    out_ref, grad_rows_ref, refs = refs[0], refs[1], refs[2:]
    grad_gu_refs, grad_d_refs, refs = refs[0:4:2], refs[1:4:2], refs[4:]
    w_gu_ref, w_d_ref, act_ref, grad_act_ref = refs
    step = pl.program_id(0)
    count = rows_ref.shape[0]
    per_part = pl.num_programs(0) // 2
    device_cols, device_rows = rings * col_rows, rings * piece
    together = w_d_ref.shape[0] // device_rows

    @pl.when(step == 0)
    def _():
        out_ref[...] = jnp.zeros_like(out_ref)
        grad_rows_ref[...] = jnp.zeros_like(grad_rows_ref)

    def place(gu_ref, d_ref, device):
        for ring in range(rings):
            first = pl.multiple_of(device * device_cols + ring * col_rows, 16)
            for column in range(w_gu_ref.shape[1] // 256):
                w_gu_ref[pl.ds(first, col_rows), column * 256 : (column + 1) * 256] = gu_ref[
                    ring, column * col_rows : (column + 1) * col_rows, :
                ]

        @pl.when(device // together == step % per_part)
        def _():
            for ring in range(rings):
                first = pl.multiple_of(device % together * device_rows + ring * piece, 16)
                for column in range(w_d_ref.shape[1] // 256):
                    w_d_ref[pl.ds(first, piece), column * 256 : (column + 1) * 256] = d_ref[
                        ring, column * piece : (column + 1) * piece, :
                    ]

    for part in range(2):

        @pl.when(step // per_part == part)
        def _():
            for index in range(partners):
                at = 2 * (part * partners + index)
                place(stacks[at], stacks[at + 1], here_ref[0] ^ index)

    def rows_of(block):
        rows = slice(block * ROW_BLOCK, (block + 1) * ROW_BLOCK)
        return rows, rows_ref[rows, :], grad_ref[rows, :]

    swiglu_blocks(
        count // ROW_BLOCK, rows_of, w_gu_ref, w_d_ref, act_ref, grad_act_ref, out_ref,
        grad_rows_ref,
    )
    grad_gu = dot_nn(side_by_side(rows_t_ref), grad_act_ref[...]).astype(LOW)
    grad_d = dot_nn(side_by_side(grad_t_ref), act_ref[...]).astype(LOW).T
    for part in range(2):

        @pl.when(step // per_part == part)
        def _():
            grad_gu_refs[part][...] = grad_gu
            grad_d_refs[part][...] = grad_d


def swiglu_stacks(
    here, rows, grad, rows_t, grad_t, near, far, rings, col_rows, piece, after
):
    count, width = rows.shape
    partners = len(near)
    chunk = EXPERT_BLOCK
    hidden = partners * rings * piece
    per_part = hidden // chunk
    gu_tall, d_tall = 2 * chunk // 256 * col_rows, width // 256 * piece
    assert gu_tall * per_part % d_tall == 0

    def place(part):
        return lambda step: jnp.clip(step - part * per_part, 0, per_part - 1)

    operands, stack_specs, out_specs = [], [], []
    for part, stacks in enumerate((near, far)):
        for stack in stacks:
            operands += [stack.reshape(rings, -1, 256)] * 2
            stack_specs += [
                pl.BlockSpec(
                    (rings, gu_tall, 256), lambda step, at=place(part): (0, at(step), 0)
                ),
                pl.BlockSpec(
                    (rings, d_tall, 256),
                    lambda step: (0, gu_tall * per_part // d_tall, 0),
                    pipeline_mode=pl.Buffered(1),
                ),
            ]
        out_specs += [
            pl.BlockSpec((width, 2 * chunk), lambda step, at=place(part): (0, at(step))),
            pl.BlockSpec((chunk, width), lambda step, at=place(part): (at(step), 0)),
        ]
    kernel = functools.partial(swiglu_stacks_kernel, partners, rings, col_rows, piece)
    return pl.pallas_call(
        ignoring(kernel, 5 + 4 * partners, len(after)),
        grid=(2 * per_part,),
        out_shape=[jax.ShapeDtypeStruct((count, width), WIDE)] * 2
        + [
            jax.ShapeDtypeStruct((width, 2 * hidden), LOW),
            jax.ShapeDtypeStruct((hidden, width), LOW),
        ]
        * 2,
        in_specs=[pl.BlockSpec(memory_space=pltpu.SMEM)]
        + [once(each.shape) for each in (rows, grad, rows_t, grad_t)]
        + stack_specs
        + [ANYWHERE] * len(after),
        out_specs=[whole((count, width))] * 2 + out_specs,
        scratch_shapes=[
            pltpu.VMEM((width, 2 * chunk), LOW),
            pltpu.VMEM((chunk, width), LOW),
            pltpu.VMEM((count, chunk), LOW),
            pltpu.VMEM((count, 2 * chunk), LOW),
        ],
        compiler_params=params(),
        cost_estimate=pl.CostEstimate(
            flops=36 * count * width * hidden,
            bytes_accessed=24 * width * hidden + 12 * count * width,
            transcendentals=2 * count * hidden,
        ),
    )(here, rows, grad, rows_t, grad_t, *operands, *after)


def pack_grads_kernel(rings, col_rows, piece, here_ref, *refs):
    grad_refs, out_refs = refs[:4], refs[4:]

    def place(out_ref):
        for ring in range(rings):
            first = 0
            for near, far, rows in ((*grad_refs[:2], col_rows), (*grad_refs[2:], piece)):
                for column in range(near.shape[1] // 256):
                    part = (
                        slice(ring * rows, (ring + 1) * rows),
                        slice(column * 256, (column + 1) * 256),
                    )
                    out_ref[ring, first : first + rows, :] = (
                        near[part].astype(WIDE) + far[part].astype(WIDE)
                    ).astype(LOW)
                    first += rows

    for index, out_ref in enumerate(out_refs):
        pl.when(pl.program_id(0) == index)(functools.partial(place, out_ref))


def pack_grads(here, partners, near, far, rings, col_rows, piece):
    grads = [near[0], far[0], near[1], far[1]]
    specs = [
        pl.BlockSpec(
            (grad.shape[0] // partners, grad.shape[1]), lambda step, here: (here[0] ^ step, 0)
        )
        for grad in grads
    ]
    rows = sum(grad.shape[0] // partners * grad.shape[1] for grad in grads[::2]) // (256 * rings)
    shape = (rings, rows, 256)
    outs = pl.pallas_call(
        functools.partial(pack_grads_kernel, rings, col_rows, piece),
        grid_spec=pltpu.PrefetchScalarGridSpec(
            num_scalar_prefetch=1,
            grid=(partners,),
            in_specs=specs,
            out_specs=[whole(shape)] * partners,
        ),
        out_shape=[jax.ShapeDtypeStruct(shape, LOW)] * partners,
        compiler_params=params(),
        cost_estimate=pl.CostEstimate(flops=0, bytes_accessed=20_000_000, transcendentals=0),
    )(here, *grads)
    return [out.reshape(rings * rows, 256) for out in outs]


def adam_update(weight, first_state, second_state, gradient, step_rate, decay_rate):
    first_new = FIRST_BETA * first_state + (1.0 - FIRST_BETA) * gradient
    second_new = SECOND_BETA * second_state + (1.0 - SECOND_BETA) * gradient * gradient
    first_hat = first_new / (1.0 - FIRST_BETA**STEP)
    second_hat = second_new / (1.0 - SECOND_BETA**STEP)
    weight_new = weight - step_rate * (
        first_hat / (jnp.sqrt(second_hat) + ADAM_EPSILON) + decay_rate * weight
    )
    return (weight_new, first_new, second_new)


def update_kind(state_refs, new_refs, gradient):
    updated = adam_update(*(ref[0] for ref in state_refs), gradient, RATE_MATRIX, WEIGHT_DECAY)
    for ref, value in zip(new_refs, updated):
        ref[0] = value


def expert_update_kernel(gu_ref, down_ref, *refs):
    state_refs, new_refs, rows_ref = refs[:3], refs[3:6], refs[6]

    def one_kind(kind):
        grad_ref = gu_ref if kind < 2 else down_ref
        columns = state_refs[0].shape[1] // grad_ref.shape[0]
        for column in range(columns):
            left = column * 128
            if kind < 2:
                left = (column // 2 * 2 + kind) * 256 + column % 2 * 128
            rows_ref[pl.ds(column, grad_ref.shape[0], stride=columns), :] = grad_ref[
                :, left : left + 128
            ].astype(WIDE)
        update_kind(state_refs, new_refs, rows_ref[...])

    for kind in range(3):
        pl.when(pl.program_id(0) == kind)(functools.partial(one_kind, kind))


def shared_update_kernel(own_rows, piece, grad_ref, *refs):
    state_refs, new_refs, wide_ref, rows_ref = refs[:3], refs[3:6], refs[6], refs[7]
    blocks = FFS // 256

    def gate_or_up(kind):
        columns = FFS // 128
        lane = lax.broadcasted_iota(jnp.int32, (own_rows, 128), 1)
        for column in range(columns):
            unit = column * piece
            left = unit % 256 // 128 * 128
            low, high = (
                wide_ref[pl.ds((half * blocks + unit // 256 * 2 + kind) * own_rows, own_rows),
                         left : left + 128]
                for half in range(2)
            )
            if unit % 128:
                low = pltpu.roll(low, 64, 1)
            else:
                high = pltpu.roll(high, 64, 1)
            rows_ref[pl.ds(column, own_rows, stride=columns), :] = jnp.where(
                lane < piece, low, high
            )

    def down():
        columns = HEADS * HEAD_DIM // 128
        for column in range(columns):
            first = 2 * blocks * own_rows + column // 2 * piece
            left = column % 2 * 128
            rows_ref[pl.ds(column, piece, stride=columns), :] = wide_ref[
                first : first + piece, left : left + 128
            ]

    @pl.when(pl.program_id(0) == 0)
    def _():
        wide_ref[...] = grad_ref[...].astype(WIDE)

    for kind, place in enumerate(
        (functools.partial(gate_or_up, 0), functools.partial(gate_or_up, 1), down)
    ):

        @pl.when(pl.program_id(0) == kind)
        def _():
            place()
            update_kind(state_refs, new_refs, rows_ref[...])


def update(kernel, grads, states, scratch):
    kinds, rows, _ = states[0].shape
    block = pl.BlockSpec((1, rows, 128), lambda kind: (kind, 0, 0))
    return pl.pallas_call(
        kernel,
        grid=(kinds,),
        out_shape=[jax.ShapeDtypeStruct(states[0].shape, WIDE)] * 3,
        in_specs=[once(grad.shape) for grad in grads] + [block] * 3,
        out_specs=[block] * 3,
        scratch_shapes=scratch + [pltpu.VMEM((rows, 128), WIDE)],
        compiler_params=params(),
        cost_estimate=AT_ONCE,
    )(*grads, *states)


def expert_update(gu, down, states):
    return update(expert_update_kernel, [gu, down], states, [])


def shared_update(grad, own_rows, piece, states):
    kernel = functools.partial(shared_update_kernel, own_rows, piece)
    return update(kernel, [grad], states, [pltpu.VMEM(grad.shape, WIDE)])


def slot_place(owners, own_count, owner_count):
    onehot = (owners[:, None] == jnp.arange(owner_count, dtype=jnp.int32)[None, :]).astype(
        jnp.int32
    )
    prior_count = jnp.sum((jnp.cumsum(onehot, 0) - onehot) * onehot, 1)
    return owners * own_count + prior_count


def rope_tables(length):
    inv_freq = ROPE_BASE ** (-(jnp.arange(HALF, dtype=WIDE) * 2.0 / HEAD_DIM))
    phase_angle = jnp.arange(length, dtype=WIDE)[:, None] * inv_freq[None, :]
    return (jnp.tile(jnp.cos(phase_angle), (1, PACK)), jnp.tile(jnp.sin(phase_angle), (1, PACK)))


def rms_scale(values):
    return lax.rsqrt(jnp.mean(values * values, -1, keepdims=True) + NORM_EPSILON)


def norm_back(grad_normed, hat_values, rms_values, gain):
    grad_hat = grad_normed * gain
    return rms_values * (grad_hat - hat_values * jnp.mean(grad_hat * hat_values, -1, keepdims=True))


SHARD = ("ring", "core")
EVERY = ("expert", "ring", "core")


def to_partner(value, axis, distance):
    size = lax.axis_size(axis)
    return lax.ppermute(value, axis, [(index, index ^ distance) for index in range(size)])


def exchange(values, axis):
    return [values[0]] + [
        to_partner(value, axis, distance) for distance, value in enumerate(values) if distance
    ]


def collect(value, axis):
    return exchange([value] * lax.axis_size(axis), axis)


def add_up(value, axes):
    for axis in axes:
        distance = 1
        while distance < lax.axis_size(axis):
            value = value + to_partner(value, axis, distance)
            distance *= 2
    return value


def gather_rows(part, axes):
    return lax.all_gather(part, axes, axis=0, tiled=True)


def scatter_rows(grad, axes):
    return lax.psum_scatter(grad, axes, scatter_dimension=0, tiled=True)


def to_sibling(value):
    return to_partner(value, "core", 1)


def sum_low(parts):
    return sum((part.astype(WIDE) for part in parts[1:]), parts[0].astype(WIDE)).astype(LOW)


def interleave(gate, up):
    rows, hidden = gate.shape
    blocks = (rows, hidden // HIDDEN_BLOCK, HIDDEN_BLOCK)
    return jnp.concatenate([gate.reshape(blocks), up.reshape(blocks)], 2).reshape(rows, 2 * hidden)


def deinterleave(both):
    rows, columns = both.shape
    blocks = both.reshape(rows, columns // (2 * HIDDEN_BLOCK), 2 * HIDDEN_BLOCK)
    return (
        blocks[:, :, :HIDDEN_BLOCK].reshape(rows, columns // 2),
        blocks[:, :, HIDDEN_BLOCK:].reshape(rows, columns // 2),
    )


def by_core(columns, piece):
    rows, hidden = columns.shape
    return (
        columns.reshape(rows, hidden // (2 * piece), 2, piece)
        .transpose(0, 2, 1, 3)
        .reshape(rows, 2, hidden // 2)
    )


def from_core(columns, piece):
    rows, _, half = columns.shape
    return (
        columns.reshape(rows, 2, half // piece, piece).transpose(0, 2, 1, 3).reshape(rows, 2 * half)
    )


def pack(columns, rows):
    return jnp.concatenate(
        [
            part.reshape(part.shape[0], -1, 256).transpose(1, 0, 2).reshape(-1, 256)
            for part in (columns, rows)
        ],
        0,
    )


def unpack(stack, col_rows, piece):
    per_device = FFS // 256 * col_rows
    stack = stack.reshape(-1, per_device + piece * HEADS * HEAD_DIM // 256, 256)
    devices = stack.shape[0]
    return [
        part.reshape(devices, -1, rows, 256)
        .transpose(0, 2, 1, 3)
        .reshape(devices * rows, -1)
        for part, rows in ((stack[:, :per_device], col_rows), (stack[:, per_device:], piece))
    ]


def body(
    tokens_in,
    cotangent,
    routes,
    prefix,
    owners,
    attn_master,
    attn_first,
    attn_second,
    expert_master,
    expert_first,
    expert_second,
    shared_master,
    shared_first,
    shared_second,
    norm_gains,
    gains_first,
    gains_second,
    router,
    router_first,
    router_second,
):
    tok_count, model_width = tokens_in.shape
    owner_count = lax.axis_size("expert")
    own_count = attn_master.shape[0]
    experts_all = router.shape[1]
    top_count = routes.shape[1]
    capacity = tok_count * top_count // experts_all

    here = lax.axis_index("expert")
    here_ref = here.astype(jnp.int32)[None]
    core = lax.axis_index("core")
    rings = lax.axis_size("ring")
    slot_of = slot_place(owners, own_count, owner_count)
    slot_of = (slot_of // own_count ^ here) * own_count + slot_of % own_count
    attn_cols = gather_columns(
        jnp.concatenate(collect(attn_master.astype(LOW), "expert"), 0), slot_of
    )
    w_attn = gather_rows(attn_cols, SHARD)
    expert_columns = interleave(
        expert_master[0, 0].reshape(-1, FF).astype(LOW),
        expert_master[0, 1].reshape(-1, FF).astype(LOW),
    )
    expert_rows = expert_master[0, 2].reshape(-1, model_width).astype(LOW)
    expert_stack = gather_rows(pack(expert_columns, expert_rows)[None], SHARD)
    shared_down = shared_master[2].reshape(-1, model_width).astype(LOW)
    piece = shared_down.shape[0]
    gate_cols = by_core(shared_master[0].reshape(-1, FFS).astype(LOW), piece)
    up_cols = by_core(shared_master[1].reshape(-1, FFS).astype(LOW), piece)
    halves = [interleave(gate_cols[:, half], up_cols[:, half]) for half in range(2)]
    shared_rows = 2 * halves[0].shape[0]
    own_half = jnp.where(core == 0, halves[0], halves[1])
    far_half = to_sibling(jnp.where(core == 0, halves[1], halves[0]))
    near_gu = jnp.where(
        core == 0,
        jnp.concatenate([own_half, far_half], 0),
        jnp.concatenate([far_half, own_half], 0),
    )
    shared_packs = collect(gather_rows(pack(near_gu, shared_down), "ring"), "expert")
    whole_tiles = shared_rows % 16 == 0 and piece % 16 == 0

    router_low = router.astype(LOW)
    flat_ids = routes.reshape(-1)
    onehot = (flat_ids[:, None] == jnp.arange(experts_all, dtype=jnp.int32)[None, :]).astype(
        jnp.int32
    )
    slot_rank = jnp.sum((jnp.cumsum(onehot, 0) - onehot) * onehot, 1)
    target_row = jnp.where(
        slot_rank < capacity, flat_ids * capacity + slot_rank, experts_all * capacity
    ).reshape(tok_count, top_count)
    router_rows = jnp.zeros((128, model_width), LOW).at[:experts_all].set(router_low.T)

    cos, sin = rope_tables(tok_count)
    target_t = target_row.T
    query, key, value, heads, rest, totals, normed, middle, branch_in = attend_forward(
        prefix, tokens_in, norm_gains, cos, sin, w_attn, [target_t, router_rows]
    )

    first_send, second_send, branch_t, cotangent_t = dispatch(
        here_ref, routes.T, target_t, branch_in, cotangent, router_rows[:16], owner_count,
        capacity,
    )
    first_rows = exchange(first_send, "expert")
    second_rows = exchange(second_send, "expert")
    turned_pair = [branch_in, cotangent, branch_t, cotangent_t]
    if whole_tiles:
        near_packs = wait_all(shared_packs, totals)
        far_packs = [to_sibling(stack) for stack in near_packs]
        shared_outs = swiglu_stacks(
            here_ref, *turned_pair, near_packs, far_packs, rings, shared_rows, piece, []
        )
    else:
        order = jnp.arange(owner_count) ^ here
        w_sgu, w_sd = unpack(
            jnp.take(jnp.stack(shared_packs), order, axis=0), shared_rows, piece
        )
        shared_outs = swiglu(
            *turned_pair, [w_sgu, to_sibling(w_sgu)], [w_sd, to_sibling(w_sd)]
        )
    shared_out, grad_branch_shared, grad_sgu, grad_sd, grad_sgu_far, grad_sd_far = shared_outs
    first_out, first_act, first_grad_act, first_turned = expert_pass(
        first_rows, expert_stack, [grad_branch_shared]
    )
    first_back = exchange(first_out, "expert")
    second_out, second_act, second_grad_act, second_turned = expert_pass(
        second_rows, expert_stack, [first_act]
    )
    second_back = exchange(second_out, "expert")
    far = [to_sibling(grad_sgu_far), to_sibling(grad_sd_far)]
    if whole_tiles:
        packs = pack_grads(
            here_ref, owner_count, [grad_sgu, grad_sd], far, rings, shared_rows, piece
        )
    else:
        pair_gu, pair_down = sum_low([grad_sgu, far[0]]), sum_low([grad_sd, far[1]])
        stacks = jnp.concatenate(
            [
                pack(
                    pair_gu[device * shared_rows : (device + 1) * shared_rows],
                    pair_down[device * piece : (device + 1) * piece],
                )
                for device in range(owner_count * rings)
            ],
            0,
        ).reshape(owner_count, -1, 256)
        stacks = jnp.take(stacks, order, axis=0)
        packs = [stacks[index] for index in range(owner_count)]
    turned = [first_turned, second_turned]
    grad_ed = weight_grad(turned, [first_act, second_act], 1, True, 512, first_back[1:])
    expert_down_low = scatter_rows(grad_ed, SHARD)
    grad_egu = weight_grad(
        turned, [first_grad_act, second_grad_act], 0, False, 1024, [grad_ed]
    )
    expert_gu_low = scatter_rows(grad_egu, SHARD)

    packs = wait_all(packs, grad_egu, *second_back[1:])
    (
        block_out, grad_middle, grad_attn_low, grad_attn_t, normed_t, grad_router_rows,
        grad_gain_rows,
    ) = combine(
        here_ref, routes, target_row, first_back, second_back, middle, shared_out,
        grad_branch_shared, cotangent, branch_in, normed, norm_gains, router_rows,
        [grad_egu, packs[0]],
    )

    grad_w, grad_normed = attend_backward(
        prefix, query, key, value, heads, rest, totals, cos, sin, normed_t, grad_attn_low,
        grad_attn_t, w_attn,
    )
    quarters = exchange(packs, "expert")
    attn_sum = scatter_rows(
        wait_for(grad_w, expert_gu_low, expert_down_low, *quarters[1:]), SHARD
    )
    quarter = sum_low(quarters).reshape(rings, -1, 256)
    blocks = FFS // 256
    columns = quarter[:, : blocks * shared_rows].reshape(
        rings, blocks, 2, shared_rows // 2, 256
    )
    mine = jnp.where(core == 0, columns[:, :, 0], columns[:, :, 1])
    other = to_sibling(jnp.where(core == 0, columns[:, :, 1], columns[:, :, 0]))
    by_half = [jnp.where(core == half, mine, other) for half in range(2)]
    quarter = jnp.concatenate(
        [half.reshape(rings, -1, 256) for half in by_half]
        + [quarter[:, blocks * shared_rows :]],
        1,
    ).reshape(-1, 256)
    hidden_in = tokens_in.astype(WIDE)
    first_rms = rms_scale(hidden_in)
    first_hat = hidden_in * first_rms
    grad_first_gain = jnp.sum(grad_normed * first_hat, 0)
    tokens_grad = grad_middle + norm_back(grad_normed, first_hat, first_rms, norm_gains[0])

    small = jnp.concatenate(
        [
            grad_first_gain[None],
            jnp.sum(grad_gain_rows, 0, keepdims=True),
            grad_router_rows[:experts_all],
        ],
        0,
    )
    small_sum = add_up(small, EVERY)
    gain_grad = small_sum[:2]
    router_grad = small_sum[2:].T

    expert_new, expert_first_new, expert_second_new = (
        state[None]
        for state in expert_update(
            expert_gu_low,
            expert_down_low,
            [state[0] for state in (expert_master, expert_first, expert_second)],
        )
    )
    gains_new, gains_first_new, gains_second_new = adam_update(
        norm_gains, gains_first, gains_second, gain_grad, RATE_GAIN, 0.0
    )
    router_new, router_first_new, router_second_new = adam_update(
        router, router_first, router_second, router_grad, RATE_ROUTER, WEIGHT_DECAY
    )
    owned_count = jnp.sum((owners == lax.axis_index("expert")).astype(jnp.int32))
    slot_held = (jnp.arange(own_count, dtype=jnp.int32) < owned_count).astype(jnp.int32)
    quarter, attn_sum, slot_held = wait_all(
        [quarter, attn_sum, slot_held], gains_new, tokens_grad, expert_new
    )
    shared_low = scatter_rows(quarter, "ring")
    slot_grads = split_columns(attn_sum, slot_of, owner_count, own_count)
    owned_grad = sum(part.astype(WIDE) for part in exchange(slot_grads, "expert"))

    slot_used = (slot_held > 0)[:, None, None]
    attn_w, attn_m, attn_n = adam_update(
        attn_master, attn_first, attn_second, owned_grad, RATE_ATTENTION, WEIGHT_DECAY
    )
    attn_new = jnp.where(slot_used, attn_w, 0.0)
    attn_first_new = jnp.where(slot_used, attn_m, 0.0)
    attn_second_new = jnp.where(slot_used, attn_n, 0.0)
    own_rows = shared_rows // 2
    shared_states = [shared_master, shared_first, shared_second]
    if whole_tiles and piece == 64 and own_rows % 8 == 0:
        shared_new, shared_first_new, shared_second_new = shared_update(
            shared_low, own_rows, piece, shared_states
        )
    else:
        top = 2 * blocks * own_rows
        by_half = (
            shared_low[:top]
            .reshape(2, blocks, own_rows, 256)
            .transpose(0, 2, 1, 3)
            .reshape(2, own_rows, FFS)
            .astype(WIDE)
        )
        parts = [deinterleave(by_half[half]) for half in range(2)]
        down = shared_low[top:].reshape(-1, piece, 256).transpose(1, 0, 2).astype(WIDE)
        shared_summed = jnp.stack(
            [
                from_core(jnp.stack([parts[0][kind], parts[1][kind]], 1), piece).reshape(-1, 128)
                for kind in range(2)
            ]
            + [down.reshape(-1, 128)]
        )
        shared_new, shared_first_new, shared_second_new = adam_update(
            *shared_states, shared_summed, RATE_MATRIX, WEIGHT_DECAY
        )
    copies = jnp.concatenate(collect(attn_new.astype(LOW), "expert"), 0)
    attn_copy = jnp.take(wait_for(copies, shared_new), slot_of, axis=0)
    return (
        block_out,
        tokens_grad,
        attn_new,
        attn_first_new,
        attn_second_new,
        attn_copy,
        expert_new,
        expert_first_new,
        expert_second_new,
        shared_new,
        shared_first_new,
        shared_second_new,
        gains_new,
        gains_first_new,
        gains_second_new,
        router_new,
        router_first_new,
        router_second_new,
    )


def solution(mesh):
    owner_count, shard_count = mesh.devices.shape
    fine = Mesh(mesh.devices.reshape(owner_count, shard_count // 2, 2), EVERY)
    tokens = P(EVERY, None)
    slots = P("expert", SHARD, None)
    experts = P("expert", None, SHARD, None)
    shared = P(None, EVERY, None)
    return jax.shard_map(
        body,
        mesh=fine,
        in_specs=(tokens,) * 3
        + (P(EVERY), P())
        + (slots,) * 3
        + (experts,) * 3
        + (shared,) * 3
        + (P(),) * 6,
        out_specs=(tokens,) * 2
        + (slots,) * 3
        + (P(None, SHARD, None),)
        + (experts,) * 3
        + (shared,) * 3
        + (P(),) * 6,
        check_vma=False,
    )
```
